256 devices in a mesh: group: 16 (over z, core), tensor: 4 (over x), seq: 4 (over y).
Axes of the slice: x: 4, y: 4, z: 8, core: 2. Of those that a mesh axis runs over, the one named last changes fastest.
Arguments:
- hidden: bfloat16 [4096, 8192], P('group', ('tensor', 'seq')), may hold values from -6 to 6
- key_value_weight: bfloat16 [8192, 8, 2, 128], P(('tensor', 'seq')), may hold values from -0.0625 to 0.0625
- adapter_down_weight: bfloat16 [64, 8192, 128], P('group', ('tensor', 'seq')), may hold values from -0.0625 to 0.0625
- adapter_up_weight: bfloat16 [64, 2, 64, 1024], P('group', None, None, 'tensor'), may hold values from -0.75 to 0.75
- queries: bfloat16 [4096, 8192], P('group', 'tensor'), may hold values from -120 to 120
- key_value_cache: bfloat16 [32, 16384, 8, 2, 128], P('group', 'seq', 'tensor'), may hold values from -6.08 to 6.08
- request_adapter: int32 [32], replicated, may hold values from 0 to 63
Outputs:
- new_kv: bfloat16 [4096, 8, 2, 128], P(('group', 'seq'), 'tensor')
- attention: bfloat16 [4096, 8192], P(('group', 'seq'), 'tensor')
The draws below stay inside these ranges and needn't reach their ends.
All inputs are finite; a program needn't handle non-finite values.
Results may differ from the reference program's by a relative error of at most 0.012.
Values may be sent and summed in bfloat16 or wider, within the bound.
No kernel may reach another device: no remote copies, remote signals or barrier semaphores. Data moves between devices by JAX's collectives and lax.ppermute only.
A program may use at most 192 MiB of HBM per device.

```python
import math
import jax
import jax.numpy as jnp
import numpy as np
from jax import lax

MODEL_WIDTH = 8192
HEADS = 64
KEY_VALUE_HEADS = 8
HEAD_WIDTH = 128
ADAPTER_RANK = 64
NEW_TOK = 128
CACHE = 16384
ADAPTER_COUNT = 64
REQUESTS = 32
TOKEN_TOTAL = 4096


def cache_start(key):
    return jax.random.truncated_normal(key, -6.0, 6.0, (REQUESTS, KEY_VALUE_HEADS, 2, HEAD_WIDTH), jnp.float32)


def draw_key_value_cache(key, part):
    leading = cache_start(key)
    key = jax.random.fold_in(key, 3)
    remaining = jax.random.truncated_normal(key, -6.0, 6.0, (REQUESTS, CACHE - 1, KEY_VALUE_HEADS, 2, HEAD_WIDTH), jnp.float32)
    whole = jnp.concatenate([leading[:, None], remaining], axis=1)
    return whole.astype(jnp.bfloat16)


def draw_queries(key, part):
    key = jax.random.fold_in(key, 5)
    drawn = jax.random.truncated_normal(key, -6.0, 6.0, (REQUESTS, NEW_TOK, HEADS * HEAD_WIDTH), jnp.float32)
    return drawn.reshape(TOKEN_TOTAL, HEADS * HEAD_WIDTH).astype(jnp.bfloat16)


def with_ends(values, own_key, low, largest):
    longest = values.shape.index(max(values.shape))
    spots = []
    for shift in (0, 1):
        where = [jax.random.randint(jax.random.fold_in(own_key, axis), (), 0, length) for axis, length in enumerate(values.shape)]
        where[longest] = (where[longest] + shift) % values.shape[longest]
        spots.append(tuple(where))
    return values.at[spots[0]].set(low).at[spots[1]].set(largest)


def level_of(key, shape, split, least, largest):
    level, own = 1.0, jax.random.fold_in(key, 6)
    for position, shards_of in split:
        draws = jnp.exp(jax.random.uniform(jax.random.fold_in(own, position), (shards_of,), jnp.float32, least / len(split), largest / len(split)))
        level = level * jnp.repeat(draws, shape[position] // shards_of).reshape([-1 if axis == position else 1 for axis in range(len(shape))])
    return level


def rank_bounds(amount, skew):
    weights = [(1 << 20) // math.isqrt(rank ** skew) + 1 for rank in range(1, amount + 1)]
    deviation = 1 + sum(weights) // (1 << 30)
    return np.cumsum(np.array([max(1, weight // deviation) for weight in weights]))


def ranked_ids(stream_key, dims, amount, skew):
    listing = rank_bounds(amount, skew)
    pick = jax.random.randint(jax.random.fold_in(stream_key, 1), dims, 0, int(listing[amount - 1]))
    grade = jnp.searchsorted(jnp.asarray(listing, jnp.int32), pick, side="right")
    return jax.random.permutation(jax.random.fold_in(stream_key, 2), amount)[grade].astype(jnp.int32)


def gaussian(stream_key, shape, deviation, bound, pieces=(), held_as=jnp.bfloat16):
    entries = jax.random.normal(stream_key, shape, jnp.float32) * deviation
    if len(pieces) > 0:
        entries = level_of(stream_key, shape, pieces, -0.22, 0.18) * entries
    return jnp.clip(entries, min=-bound, max=bound).astype(held_as)


def setup_inputs(seed: int = 0) -> dict:
    streams_of = jax.random.split(jax.random.key(seed), 8)
    return {
        "hidden": gaussian(streams_of[0], (TOKEN_TOTAL, MODEL_WIDTH), 1.0, 6.0, ((0, 16), (1, 16))),
        "key_value_weight": gaussian(streams_of[1], (MODEL_WIDTH, KEY_VALUE_HEADS, 2, HEAD_WIDTH), MODEL_WIDTH ** -0.5, 0.0625, ((0, 16),)),
        "adapter_down_weight": gaussian(streams_of[2], (ADAPTER_COUNT, MODEL_WIDTH, 2 * ADAPTER_RANK), MODEL_WIDTH ** -0.5, 0.0625, ((0, 16), (1, 16))),
        "adapter_up_weight": gaussian(streams_of[3], (ADAPTER_COUNT, 2, ADAPTER_RANK, KEY_VALUE_HEADS * HEAD_WIDTH), ADAPTER_RANK ** -0.5, 0.75, ((0, 16), (3, 4))),
        "queries": draw_queries(jax.random.fold_in(streams_of[7], 71), 0),
        "key_value_cache": draw_key_value_cache(jax.random.fold_in(streams_of[7], 71), 0),
        "request_adapter": with_ends(ranked_ids(streams_of[6], (REQUESTS,), ADAPTER_COUNT, 2), jax.random.fold_in(streams_of[6], 3), 0, ADAPTER_COUNT - 1).astype(jnp.int32),
    }


def rotate(field, positions):
    half_dim = field.shape[-1] // 2
    exponents = jnp.arange(half_dim, dtype=jnp.float32)
    frequency = jnp.exp(exponents * (-2.0 * math.log(500000.0) / field.shape[-1]))
    angles = positions.astype(jnp.float32)[:, None, None] * frequency[None, None, :]
    cos_table = jnp.cos(angles)
    sin_table = jnp.sin(angles)
    upper_half = field[..., :half_dim]
    lower_half = field[..., half_dim:]
    return jnp.concatenate([upper_half * cos_table - lower_half * sin_table, lower_half * cos_table + upper_half * sin_table], axis=-1)

def reference(hidden, key_value_weight, adapter_down_weight, adapter_up_weight, queries, key_value_cache, request_adapter):
    base_key_value = jnp.dot(hidden, key_value_weight.reshape(MODEL_WIDTH, KEY_VALUE_HEADS * 2 * HEAD_WIDTH), preferred_element_type=jnp.float32)
    base_key_value = base_key_value.reshape(TOKEN_TOTAL, KEY_VALUE_HEADS, 2, HEAD_WIDTH)
    per_request_rows = hidden.reshape(REQUESTS, NEW_TOK, MODEL_WIDTH)

    def apply_adapters(packed):
        token_rows, adapter_number = packed
        down_weight_block = lax.dynamic_index_in_dim(adapter_down_weight, adapter_number, 0, keepdims=False)
        up_weight_block = lax.dynamic_index_in_dim(adapter_up_weight, adapter_number, 0, keepdims=False)
        rank_vec = jnp.dot(token_rows, down_weight_block, preferred_element_type=jnp.float32).astype(jnp.bfloat16)
        rank_vec = lax.optimization_barrier(rank_vec).astype(jnp.float32).reshape(NEW_TOK, 2, ADAPTER_RANK)
        return jnp.einsum('tej,ejc->tec', rank_vec, up_weight_block.astype(jnp.float32))
    adapter_delta = lax.map(apply_adapters, (per_request_rows, request_adapter))
    adapter_delta = adapter_delta.reshape(TOKEN_TOTAL, 2, KEY_VALUE_HEADS, HEAD_WIDTH).transpose(0, 2, 1, 3)
    delta_sum = base_key_value + adapter_delta
    positions = CACHE + jnp.arange(TOKEN_TOTAL, dtype=jnp.int32) % NEW_TOK
    rotated = rotate(delta_sum[:, :, 0, :], positions)
    new_kv = jnp.stack([rotated, delta_sum[:, :, 1, :]], axis=2).astype(jnp.bfloat16)
    group_size = HEADS // KEY_VALUE_HEADS
    score_scale = 1.0 / math.sqrt(HEAD_WIDTH)
    query_all = queries.reshape(REQUESTS, NEW_TOK, KEY_VALUE_HEADS, group_size, HEAD_WIDTH)
    recent_kv = new_kv.reshape(REQUESTS, NEW_TOK, KEY_VALUE_HEADS, 2, HEAD_WIDTH)
    causal = jnp.arange(NEW_TOK)[None, :] <= jnp.arange(NEW_TOK)[:, None]

    def attend(packed):
        query_rows, cache_rows, recent_rows = packed
        query_rows = query_rows.astype(jnp.float32)
        cache_rows = cache_rows.astype(jnp.float32)
        recent_rows = recent_rows.astype(jnp.float32)
        old_scores = jnp.einsum('qgjh,pgh->qgjp', query_rows, cache_rows[:, :, 0]) * score_scale
        new_scores = jnp.einsum('qgjh,ugh->qgju', query_rows, recent_rows[:, :, 0]) * score_scale
        new_scores = jnp.where(causal[:, None, None, :], new_scores, -1e+30)
        row_top = jnp.maximum(old_scores.max(-1), new_scores.max(-1))[..., None]
        old_exp = jnp.exp(old_scores - row_top)
        new_exp = jnp.exp(new_scores - row_top)
        row_total = old_exp.sum(-1) + new_exp.sum(-1)
        old_weights = lax.optimization_barrier(old_exp.astype(jnp.bfloat16)).astype(jnp.float32)
        new_weights = lax.optimization_barrier(new_exp.astype(jnp.bfloat16)).astype(jnp.float32)
        value_sum = jnp.einsum('qgjp,pgh->qgjh', old_weights, cache_rows[:, :, 1])
        value_sum = value_sum + jnp.einsum('qgju,ugh->qgjh', new_weights, recent_rows[:, :, 1])
        return (value_sum / row_total[..., None]).reshape(NEW_TOK, HEADS * HEAD_WIDTH).astype(jnp.bfloat16)
    attention = lax.map(attend, (query_all, key_value_cache, recent_kv))
    return (new_kv, attention.reshape(TOKEN_TOTAL, HEADS * HEAD_WIDTH))
```

```python
import functools
import math

import jax
import jax.numpy as jnp
from jax import lax
from jax.experimental import pallas as pl
from jax.experimental.pallas import tpu as pltpu
from jax.sharding import PartitionSpec as P

NEW_TOK = 128
CACHE = 16384
WIDTH = 128
SCALE = math.log2(math.e) / math.sqrt(WIDTH)
KEY_BLOCK = 1024
TILE = 256
LOW = -1e30
BF = jnp.bfloat16
F32 = jnp.float32
VMEM_LIMIT = 56 * 2**20

SEQ, HALF, PARITY, TENSOR = 0, 1, 2, 3
ROW_OWN, HAS_OWN, ROW_MATE, HAS_MATE = 4, 6, 8, 10


def prep_kernel(where, hidden_ref, weight_ref, *rest):
    outs, wide = rest[:4], rest[4]
    wide[...] = weight_ref[...].astype(F32)
    depth = hidden_ref.shape[1]
    hidden = hidden_ref[...]
    for shift in range(4):
        dest = lax.rem(where[TENSOR] + shift, 4)
        cols = [
            wide[pl.ds(dest * 4 + part, depth, stride=16), :].astype(BF) for part in range(4)
        ]
        rhs = jnp.concatenate(cols, axis=1)
        outs[shift][...] = jnp.dot(hidden, rhs, preferred_element_type=F32).astype(BF)


def prep(where, hidden, weight_rows):
    tokens, depth = hidden.shape
    out = jax.ShapeDtypeStruct((tokens, 4 * WIDTH), BF)
    return pl.pallas_call(
        prep_kernel,
        grid_spec=pltpu.PrefetchScalarGridSpec(
            num_scalar_prefetch=1,
            grid=(1,),
            in_specs=[
                pl.BlockSpec(hidden.shape, lambda i, w: (0, 0)),
                pl.BlockSpec(weight_rows.shape, lambda i, w: (0, 0)),
            ],
            out_specs=[pl.BlockSpec(out.shape, lambda i, w: (0, 0))] * 4,
            scratch_shapes=[pltpu.VMEM(weight_rows.shape, F32)],
        ),
        out_shape=[out] * 4,
        compiler_params=pltpu.CompilerParams(vmem_limit_bytes=VMEM_LIMIT),
        cost_estimate=pl.CostEstimate(
            flops=2 * tokens * depth * 16 * WIDTH * 4, bytes_accessed=4 * 2**20, transcendentals=0
        ),
        name="base_partial",
    )(where, hidden, weight_rows)


def attend_kernel(
    where, q_ref, x_ref, o_first, o_second, lse_first, lse_second, acc, top, wide, keys, values
):
    block = pl.program_id(0)
    tokens = q_ref.shape[0]
    per_tile = TILE // tokens
    tiles = 8 // per_tile

    @pl.when(block == 0)
    def _():
        acc[...] = jnp.zeros_like(acc)
        top[...] = jnp.full_like(top, LOW)
        for h in range(2):
            values[h, :, WIDTH:] = jnp.ones((KEY_BLOCK, WIDTH), BF)

    wide[...] = x_ref[...].astype(F32)
    for h in range(2):
        keys[h] = wide[pl.ds(2 * h, KEY_BLOCK, stride=4), :].astype(BF)
        values[h, :, :WIDTH] = wide[pl.ds(2 * h + 1, KEY_BLOCK, stride=4), :].astype(BF)
    for h in range(2):
        for t in range(tiles):
            first = h * 8 + t * per_tile
            q = jnp.concatenate(
                [q_ref[:, (first + j) * WIDTH : (first + j + 1) * WIDTH] for j in range(per_tile)],
                axis=0,
            )
            s = (
                lax.dot_general(q, keys[h], (((1,), (1,)), ((), ())), preferred_element_type=F32)
                * SCALE
            )
            i = h * tiles + t
            before = top[i]
            after = jnp.maximum(before, jnp.max(s, axis=1, keepdims=True))
            top[i] = after
            fade = jnp.exp2(before - after)
            p = jnp.exp2(s - after[:, :1]).astype(BF)
            acc[i] = acc[i] * jnp.concatenate([fade, fade], axis=1) + jnp.dot(
                p, values[h], preferred_element_type=F32
            )

    @pl.when(block == pl.num_programs(0) - 1)
    def _():
        half = tokens // 2
        odd = where[PARITY] == 1
        lane = lax.broadcasted_iota(jnp.int32, (tokens, WIDTH), 1)
        logs = jnp.zeros((tokens, WIDTH), F32)
        for h in range(2):
            for t in range(tiles):
                i = h * tiles + t
                total = acc[i, :, WIDTH:]
                mean = (acc[i, :, :WIDTH] / total).astype(BF)
                log = top[i] + jnp.log2(total)
                for j in range(per_tile):
                    n = h * 8 + t * per_tile + j
                    early = mean[j * tokens : j * tokens + half]
                    late = mean[j * tokens + half : (j + 1) * tokens]
                    cols = slice(n * WIDTH, (n + 1) * WIDTH)
                    o_first[:, cols] = jnp.where(odd, late, early)
                    o_second[:, cols] = jnp.where(odd, early, late)
                    logs = jnp.where(lane == n, log[j * tokens : (j + 1) * tokens], logs)
        lse_first[...] = jnp.where(odd, logs[half:], logs[:half])
        lse_second[...] = jnp.where(odd, logs[:half], logs[half:])


def attend(where, queries, cache_rows, other):
    tokens, width = NEW_TOK, queries.shape[1]
    half = tokens // 2
    blocks = cache_rows.shape[0] // 2 // 4 // KEY_BLOCK
    tiles = 16 * tokens // TILE

    def request(w):
        return 1 - w[HALF] if other else w[HALF]

    o = jax.ShapeDtypeStruct((half, width), BF)
    lse = jax.ShapeDtypeStruct((half, WIDTH), F32)
    scores = 16 * tokens * blocks * KEY_BLOCK
    return pl.pallas_call(
        attend_kernel,
        grid_spec=pltpu.PrefetchScalarGridSpec(
            num_scalar_prefetch=1,
            grid=(blocks,),
            in_specs=[
                pl.BlockSpec((tokens, width), lambda i, w: (request(w), 0)),
                pl.BlockSpec((KEY_BLOCK * 4, WIDTH), lambda i, w: (request(w) * blocks + i, 0)),
            ],
            out_specs=[pl.BlockSpec(o.shape, lambda i, w: (0, 0))] * 2
            + [pl.BlockSpec(lse.shape, lambda i, w: (0, 0))] * 2,
            scratch_shapes=[
                pltpu.VMEM((tiles, TILE, 2 * WIDTH), F32),
                pltpu.VMEM((tiles, TILE, WIDTH), F32),
                pltpu.VMEM((KEY_BLOCK * 4, WIDTH), F32),
                pltpu.VMEM((2, KEY_BLOCK, WIDTH), BF),
                pltpu.VMEM((2, KEY_BLOCK, 2 * WIDTH), BF),
            ],
        ),
        out_shape=[o, o, lse, lse],
        compiler_params=pltpu.CompilerParams(vmem_limit_bytes=VMEM_LIMIT),
        cost_estimate=pl.CostEstimate(
            flops=scores * WIDTH * 8, bytes_accessed=5 * 2**20, transcendentals=scores
        ),
        name="attend_other" if other else "attend_own",
    )(where, queries, cache_rows)


def rank_kernel(where, hidden_ref, mate_ref, own_maps, mate_maps, own_out, mate_out):
    r = pl.program_id(0)
    depth = hidden_ref.shape[1]
    for rows, maps, out, flag in (
        (hidden_ref, own_maps, own_out, HAS_OWN),
        (mate_ref, mate_maps, mate_out, HAS_MATE),
    ):
        here = where[flag + r] == 1
        part = jnp.dot(rows[...], maps[0, :depth], preferred_element_type=F32).astype(BF)
        out[0, :NEW_TOK] = jnp.where(here, part, jnp.zeros_like(part))
        up = maps[0, depth:]
        out[0, NEW_TOK:] = jnp.where(here, up, jnp.zeros_like(up))


def rank_parts(where, hidden, hidden_mate, maps):
    tokens, depth = hidden.shape
    height = maps.shape[1]
    out = jax.ShapeDtypeStruct((2, NEW_TOK + height - depth, WIDTH), BF)
    out_spec = pl.BlockSpec((1,) + out.shape[1:], lambda r, w: (r, 0, 0))
    return pl.pallas_call(
        rank_kernel,
        grid_spec=pltpu.PrefetchScalarGridSpec(
            num_scalar_prefetch=1,
            grid=(2,),
            in_specs=[
                pl.BlockSpec((NEW_TOK, depth), lambda r, w: (r, 0)),
                pl.BlockSpec((NEW_TOK, depth), lambda r, w: (r, 0)),
                pl.BlockSpec((1, height, WIDTH), lambda r, w: (w[ROW_OWN + r], 0, 0)),
                pl.BlockSpec((1, height, WIDTH), lambda r, w: (w[ROW_MATE + r], 0, 0)),
            ],
            out_specs=[out_spec, out_spec],
        ),
        out_shape=[out, out],
        name="rank_partial",
    )(where, hidden, hidden_mate, maps, maps)


def pair_kernel(where, own_ref, got_ref, mine, others):
    half = where[HALF]
    mine[...] = own_ref[half] + got_ref[half]
    others[...] = own_ref[1 - half] + got_ref[1 - half]


def pair_sum(where, own, got):
    out = jax.ShapeDtypeStruct(own.shape[1:], BF)
    whole = pl.BlockSpec(memory_space=pltpu.VMEM)
    return pl.pallas_call(
        pair_kernel,
        in_specs=[pl.BlockSpec(memory_space=pltpu.SMEM), whole, whole],
        out_specs=[whole, whole],
        out_shape=[out, out],
        name="core_sum",
    )(where, own, got)


def seq_kernel(where, own, one, two, three, rank_out, up_out):
    rank = own[:NEW_TOK].astype(F32)
    for got in (one, two, three):
        rank += got[:NEW_TOK].astype(F32)
    rank_out[...] = rank.astype(BF)
    for step, got in enumerate((own, one, two, three)):
        up_out[jnp.bitwise_xor(where[SEQ], step)] = got[NEW_TOK:]


def seq_sum(where, own, got):
    whole = pl.BlockSpec(memory_space=pltpu.VMEM)
    return pl.pallas_call(
        seq_kernel,
        in_specs=[pl.BlockSpec(memory_space=pltpu.SMEM)] + [whole] * 4,
        out_specs=[whole, whole],
        out_shape=[
            jax.ShapeDtypeStruct((NEW_TOK, WIDTH), BF),
            jax.ShapeDtypeStruct((4, own.shape[0] - NEW_TOK, WIDTH), BF),
        ],
        name="seq_sum",
    )(where, own, *got)


def final_kernel(where, q_ref, cos_ref, sin_ref, up_ref, *rest):
    ranks, bases, means, logs = rest[:4], rest[4:8], rest[8:12], rest[12:16]
    kv_out, attention_out, wide = rest[16:]
    half = q_ref.shape[0]
    start = pl.multiple_of(where[PARITY] * half, half)
    rank = sum(r[...].astype(F32) for r in ranks).astype(BF)
    base = sum(b[...].astype(F32) for b in bases)
    keys, values = [], []
    for h in range(2):
        for e in range(2):
            delta = jnp.dot(
                rank[:, e * 64 : (e + 1) * 64], up_ref[2 * e + h], preferred_element_type=F32
            )
            part = 2 * h + e
            field = base[:, part * WIDTH : (part + 1) * WIDTH] + delta
            if e == 0:
                field = field * cos_ref[...] + pltpu.roll(field, WIDTH // 2, 1) * sin_ref[...]
            wide[pl.ds(part, NEW_TOK, stride=4), :] = field
            (keys, values)[e].append(field.astype(BF))
    kv_out[...] = wide[pl.ds(start * 4, half * 4), :].astype(BF)
    row = lax.broadcasted_iota(jnp.int32, (half, NEW_TOK), 0) + start
    seen = lax.broadcasted_iota(jnp.int32, (half, NEW_TOK), 1) <= row
    old_logs = [l[...] for l in logs]
    for h in range(2):
        for j in range(8):
            n = h * 8 + j
            cols = slice(n * WIDTH, (n + 1) * WIDTH)
            s = (
                lax.dot_general(
                    q_ref[:, cols], keys[h], (((1,), (1,)), ((), ())), preferred_element_type=F32
                )
                * SCALE
            )
            s = jnp.where(seen, s, LOW)
            top = jnp.max(s, axis=1, keepdims=True)
            log = [l[:, n : n + 1] for l in old_logs]
            for l in log:
                top = jnp.maximum(top, l)
            p = jnp.exp2(s - top)
            total = jnp.sum(p, axis=1, keepdims=True)
            value = jnp.dot(p.astype(BF), values[h], preferred_element_type=F32)
            for l, mean in zip(log, means):
                weight = jnp.exp2(l - top)
                total += weight
                value += weight * mean[:, cols].astype(F32)
            attention_out[:, cols] = (value / total).astype(BF)


def final(where, queries, cos, sin, up, ranks, bases, means, logs):
    half, width = means[0].shape

    def whole(a):
        return pl.BlockSpec(a.shape, lambda i, w: (0,) * a.ndim)

    rest = [cos, sin, up, *ranks, *bases, *means, *logs]
    return pl.pallas_call(
        final_kernel,
        grid_spec=pltpu.PrefetchScalarGridSpec(
            num_scalar_prefetch=1,
            grid=(1,),
            in_specs=[pl.BlockSpec((half, width), lambda i, w: (w[SEQ], 0))]
            + [whole(a) for a in rest],
            out_specs=[
                pl.BlockSpec((half * 4, WIDTH), lambda i, w: (0, 0)),
                pl.BlockSpec((half, width), lambda i, w: (0, 0)),
            ],
            scratch_shapes=[pltpu.VMEM((NEW_TOK * 4, WIDTH), F32)],
        ),
        out_shape=[
            jax.ShapeDtypeStruct((half * 4, WIDTH), BF),
            jax.ShapeDtypeStruct((half, width), BF),
        ],
        compiler_params=pltpu.CompilerParams(vmem_limit_bytes=VMEM_LIMIT),
        name="new_kv_and_merge",
    )(where, queries, *rest)


def rotary_tables():
    exponents = jnp.arange(WIDTH // 2, dtype=F32)
    frequency = jnp.exp(exponents * (-2.0 * math.log(500000.0) / WIDTH))
    positions = CACHE + jnp.arange(NEW_TOK, dtype=jnp.int32)
    angles = positions.astype(F32)[:, None] * frequency[None, :]
    cos, sin = jnp.cos(angles), jnp.sin(angles)
    return jnp.concatenate([cos, cos], axis=1), jnp.concatenate([-sin, sin], axis=1)


def flip(axis, mask):
    return lambda a: lax.ppermute(
        a, axis, [(i, i ^ mask) for i in range(lax.axis_size(axis))]
    )


def shift(axis, step):
    size = lax.axis_size(axis)
    return lambda a: lax.ppermute(a, axis, [(i, (i + step) % size) for i in range(size)])


def local(
    hidden,
    key_value_weight,
    adapter_down_weight,
    adapter_up_weight,
    queries,
    key_value_cache,
    request_adapter,
):
    seq, group, tensor = (lax.axis_index(a) for a in ("seq", "group", "tensor"))
    core = group % 2
    own_adapter = lax.dynamic_slice_in_dim(request_adapter, 2 * group, 2)
    mate_adapter = lax.dynamic_slice_in_dim(request_adapter, 2 * (group ^ 1), 2)

    def row(adapter):
        return adapter // 8 * 4 + adapter % 4

    def here(adapter):
        return (adapter // 4 % 2 == core).astype(jnp.int32)

    where = jnp.concatenate(
        [
            jnp.stack([seq, seq // 2, seq % 2, tensor]).astype(jnp.int32),
            row(own_adapter),
            here(own_adapter),
            row(mate_adapter),
            here(mate_adapter),
        ]
    )

    quarter = lax.dynamic_slice(
        adapter_up_weight, (0, seq // 2, 0, seq % 2 * WIDTH), (4, 1, 64, WIDTH)
    )
    maps = jnp.concatenate([adapter_down_weight, quarter[:, 0]], axis=1)
    same_core = [list(range(c, lax.axis_size("group"), 2)) for c in range(2)]
    maps = lax.all_gather(maps, "group", axis_index_groups=same_core, axis=0, tiled=True)
    hidden_mate = flip("group", 1)(hidden)

    parts = prep(where, hidden, key_value_weight.reshape(-1, WIDTH))
    base = parts[0].astype(F32)
    for step in (1, 2, 3):
        base += shift("tensor", step)(parts[step]).astype(F32)
    base = base.astype(BF)
    base_own = lax.dynamic_slice_in_dim(base, seq // 2 * NEW_TOK, NEW_TOK, 0)
    base_other = lax.dynamic_slice_in_dim(base, (1 - seq // 2) * NEW_TOK, NEW_TOK, 0)
    bases = [
        base_own,
        flip("seq", 1)(base_own),
        flip("seq", 2)(base_other),
        flip("seq", 3)(base_other),
    ]

    cache_rows = key_value_cache.reshape(-1, WIDTH)
    o2, o3, l2, l3 = attend(where, queries, cache_rows, True)
    o0, o1, l0, l1 = attend(where, queries, cache_rows, False)
    means = [o0, flip("seq", 1)(o1), flip("seq", 2)(o2), flip("seq", 3)(o3)]
    logs = [l0, flip("seq", 1)(l1), flip("seq", 2)(l2), flip("seq", 3)(l3)]

    own, mate = rank_parts(where, hidden, hidden_mate, maps)
    mine, others = pair_sum(where, own, flip("group", 1)(mate))
    rank, up = seq_sum(
        where, mine, [flip("seq", 1)(mine), flip("seq", 2)(others), flip("seq", 3)(others)]
    )
    ranks = [rank] + [shift("tensor", step)(rank) for step in (1, 2, 3)]

    cos, sin = rotary_tables()
    new_kv, attention = final(where, queries, cos, sin, up, ranks, bases, means, logs)
    return new_kv.reshape(-1, 2, 2, WIDTH), attention


def solution(mesh):
    in_specs = (
        P("group", ("tensor", "seq")),
        P(("tensor", "seq"), None, None, None),
        P("group", ("tensor", "seq"), None),
        P("group", None, None, "tensor"),
        P("group", "tensor"),
        P("group", "seq", "tensor", None, None),
        P(),
    )
    out_specs = (P(("group", "seq"), "tensor", None, None), P(("group", "seq"), "tensor"))
    return jax.shard_map(local, mesh=mesh, in_specs=in_specs, out_specs=out_specs, check_vma=False)
```

```python
import functools
import math

import jax
import jax.numpy as jnp
from jax import lax
from jax.experimental import pallas as pl
from jax.experimental.pallas import tpu as pltpu
from jax.sharding import PartitionSpec as P

NEW_TOK = 128
CACHE = 16384
WIDTH = 128
SCALE = math.log2(math.e) / math.sqrt(WIDTH)
KEY_BLOCK = 1024
TILE = 256
LOW = -1e30
BF = jnp.bfloat16
F32 = jnp.float32
VMEM_LIMIT = 56 * 2**20

SEQ, HALF, PARITY, TENSOR, OWN_ADAPTERS = 0, 1, 2, 3, 4


def prep_kernel(where, hidden_ref, weight_ref, *rest):
    outs, wide = rest[:4], rest[4]
    wide[...] = weight_ref[...].astype(F32)
    depth = hidden_ref.shape[1]
    hidden = hidden_ref[...]
    for shift in range(4):
        dest = lax.rem(where[TENSOR] + shift, 4)
        cols = [
            wide[pl.ds(dest * 4 + part, depth, stride=16), :].astype(BF) for part in range(4)
        ]
        rhs = jnp.concatenate(cols, axis=1)
        outs[shift][...] = jnp.dot(hidden, rhs, preferred_element_type=F32).astype(BF)


def prep(where, hidden, weight_rows):
    tokens, depth = hidden.shape
    out = jax.ShapeDtypeStruct((tokens, 4 * WIDTH), BF)
    return pl.pallas_call(
        prep_kernel,
        grid_spec=pltpu.PrefetchScalarGridSpec(
            num_scalar_prefetch=1,
            grid=(1,),
            in_specs=[
                pl.BlockSpec(hidden.shape, lambda i, w: (0, 0)),
                pl.BlockSpec(weight_rows.shape, lambda i, w: (0, 0)),
            ],
            out_specs=[pl.BlockSpec(out.shape, lambda i, w: (0, 0))] * 4,
            scratch_shapes=[pltpu.VMEM(weight_rows.shape, F32)],
        ),
        out_shape=[out] * 4,
        compiler_params=pltpu.CompilerParams(vmem_limit_bytes=VMEM_LIMIT),
        cost_estimate=pl.CostEstimate(
            flops=2 * tokens * depth * 16 * WIDTH * 4, bytes_accessed=4 * 2**20, transcendentals=0
        ),
        name="base_partial",
    )(where, hidden, weight_rows)


def attend_kernel(
    where, q_ref, x_ref, o_first, o_second, lse_first, lse_second, acc, top, wide, keys, values
):
    block = pl.program_id(0)
    tokens = q_ref.shape[0]
    per_tile = TILE // tokens
    tiles = 8 // per_tile

    @pl.when(block == 0)
    def _():
        acc[...] = jnp.zeros_like(acc)
        top[...] = jnp.full_like(top, LOW)
        for h in range(2):
            values[h, :, WIDTH:] = jnp.ones((KEY_BLOCK, WIDTH), BF)

    wide[...] = x_ref[...].astype(F32)
    for h in range(2):
        keys[h] = wide[pl.ds(2 * h, KEY_BLOCK, stride=4), :].astype(BF)
        values[h, :, :WIDTH] = wide[pl.ds(2 * h + 1, KEY_BLOCK, stride=4), :].astype(BF)
    for h in range(2):
        for t in range(tiles):
            first = h * 8 + t * per_tile
            q = jnp.concatenate(
                [q_ref[:, (first + j) * WIDTH : (first + j + 1) * WIDTH] for j in range(per_tile)],
                axis=0,
            )
            s = (
                lax.dot_general(q, keys[h], (((1,), (1,)), ((), ())), preferred_element_type=F32)
                * SCALE
            )
            i = h * tiles + t
            before = top[i]
            after = jnp.maximum(before, jnp.max(s, axis=1, keepdims=True))
            top[i] = after
            fade = jnp.exp2(before - after)
            p = jnp.exp2(s - after[:, :1]).astype(BF)
            acc[i] = acc[i] * jnp.concatenate([fade, fade], axis=1) + jnp.dot(
                p, values[h], preferred_element_type=F32
            )

    @pl.when(block == pl.num_programs(0) - 1)
    def _():
        half = tokens // 2
        odd = where[PARITY] == 1
        lane = lax.broadcasted_iota(jnp.int32, (tokens, WIDTH), 1)
        logs = jnp.zeros((tokens, WIDTH), F32)
        for h in range(2):
            for t in range(tiles):
                i = h * tiles + t
                total = acc[i, :, WIDTH:]
                mean = (acc[i, :, :WIDTH] / total).astype(BF)
                log = top[i] + jnp.log2(total)
                for j in range(per_tile):
                    n = h * 8 + t * per_tile + j
                    early = mean[j * tokens : j * tokens + half]
                    late = mean[j * tokens + half : (j + 1) * tokens]
                    cols = slice(n * WIDTH, (n + 1) * WIDTH)
                    o_first[:, cols] = jnp.where(odd, late, early)
                    o_second[:, cols] = jnp.where(odd, early, late)
                    logs = jnp.where(lane == n, log[j * tokens : (j + 1) * tokens], logs)
        lse_first[...] = jnp.where(odd, logs[half:], logs[:half])
        lse_second[...] = jnp.where(odd, logs[:half], logs[half:])


def attend(where, queries, cache_rows, other):
    tokens, width = NEW_TOK, queries.shape[1]
    half = tokens // 2
    blocks = cache_rows.shape[0] // 2 // 4 // KEY_BLOCK
    tiles = 16 * tokens // TILE

    def request(w):
        return 1 - w[HALF] if other else w[HALF]

    o = jax.ShapeDtypeStruct((half, width), BF)
    lse = jax.ShapeDtypeStruct((half, WIDTH), F32)
    scores = 16 * tokens * blocks * KEY_BLOCK
    return pl.pallas_call(
        attend_kernel,
        grid_spec=pltpu.PrefetchScalarGridSpec(
            num_scalar_prefetch=1,
            grid=(blocks,),
            in_specs=[
                pl.BlockSpec((tokens, width), lambda i, w: (request(w), 0)),
                pl.BlockSpec((KEY_BLOCK * 4, WIDTH), lambda i, w: (request(w) * blocks + i, 0)),
            ],
            out_specs=[pl.BlockSpec(o.shape, lambda i, w: (0, 0))] * 2
            + [pl.BlockSpec(lse.shape, lambda i, w: (0, 0))] * 2,
            scratch_shapes=[
                pltpu.VMEM((tiles, TILE, 2 * WIDTH), F32),
                pltpu.VMEM((tiles, TILE, WIDTH), F32),
                pltpu.VMEM((KEY_BLOCK * 4, WIDTH), F32),
                pltpu.VMEM((2, KEY_BLOCK, WIDTH), BF),
                pltpu.VMEM((2, KEY_BLOCK, 2 * WIDTH), BF),
            ],
        ),
        out_shape=[o, o, lse, lse],
        compiler_params=pltpu.CompilerParams(vmem_limit_bytes=VMEM_LIMIT),
        cost_estimate=pl.CostEstimate(
            flops=scores * WIDTH * 8, bytes_accessed=5 * 2**20, transcendentals=scores
        ),
        name="attend_other" if other else "attend_own",
    )(where, queries, cache_rows)


def rank_kernel(where, hidden_ref, maps, mine, others, held, sem):
    depth = hidden_ref.shape[1]
    copies = [
        pltpu.make_async_copy(maps.at[where[OWN_ADAPTERS + r]], held.at[r], sem.at[r])
        for r in range(2)
    ]
    for copy in copies:
        copy.start()
    parts = []
    for r in range(2):
        copies[r].wait()
        parts.append(
            jnp.dot(
                hidden_ref[r * NEW_TOK : (r + 1) * NEW_TOK],
                held[r, :depth],
                preferred_element_type=F32,
            ).astype(BF)
        )
    second = where[HALF] == 1
    ups = [held[r, depth:] for r in range(2)]
    mine[:NEW_TOK] = jnp.where(second, parts[1], parts[0])
    mine[NEW_TOK:] = jnp.where(second, ups[1], ups[0])
    others[:NEW_TOK] = jnp.where(second, parts[0], parts[1])
    others[NEW_TOK:] = jnp.where(second, ups[0], ups[1])


def rank_parts(where, hidden, maps):
    height = maps.shape[1]
    out = jax.ShapeDtypeStruct((NEW_TOK + height - hidden.shape[1], WIDTH), BF)
    whole = pl.BlockSpec(memory_space=pltpu.VMEM)
    return pl.pallas_call(
        rank_kernel,
        in_specs=[
            pl.BlockSpec(memory_space=pltpu.SMEM),
            whole,
            pl.BlockSpec(memory_space=pl.ANY),
        ],
        out_specs=[whole, whole],
        out_shape=[out, out],
        scratch_shapes=[pltpu.VMEM((2, height, WIDTH), BF), pltpu.SemaphoreType.DMA((2,))],
        compiler_params=pltpu.CompilerParams(vmem_limit_bytes=VMEM_LIMIT),
        name="rank_partial",
    )(where, hidden, maps)


def seq_kernel(where, own, one, two, three, rank_out, up_out):
    rank = own[:NEW_TOK].astype(F32)
    for got in (one, two, three):
        rank += got[:NEW_TOK].astype(F32)
    rank_out[...] = rank.astype(BF)
    for step, got in enumerate((own, one, two, three)):
        up_out[jnp.bitwise_xor(where[SEQ], step)] = got[NEW_TOK:]


def seq_sum(where, own, got):
    whole = pl.BlockSpec(memory_space=pltpu.VMEM)
    return pl.pallas_call(
        seq_kernel,
        in_specs=[pl.BlockSpec(memory_space=pltpu.SMEM)] + [whole] * 4,
        out_specs=[whole, whole],
        out_shape=[
            jax.ShapeDtypeStruct((NEW_TOK, WIDTH), BF),
            jax.ShapeDtypeStruct((4, own.shape[0] - NEW_TOK, WIDTH), BF),
        ],
        name="seq_sum",
    )(where, own, *got)


def merge_kernel(*refs):
    means, logs, mean_out, log_out = refs[:4], refs[4:8], refs[8], refs[9]
    half = means[0].shape[0]
    tops = [l[...] for l in logs]
    top = functools.reduce(jnp.maximum, tops)
    weights = [jnp.exp2(l - top) for l in tops]
    total = sum(weights)
    merged = top + jnp.log2(total)
    weights = [w / total for w in weights]
    for n in range(16):
        rows = slice(n * half, (n + 1) * half)
        cols = slice(n * WIDTH, (n + 1) * WIDTH)
        mean_out[rows] = sum(
            w[:, n : n + 1] * m[:, cols].astype(F32) for w, m in zip(weights, means)
        )
        log_out[rows] = jnp.broadcast_to(merged[:, n : n + 1], (half, WIDTH))


def merge(means, logs):
    out = jax.ShapeDtypeStruct((16 * means[0].shape[0], WIDTH), F32)
    whole = pl.BlockSpec(memory_space=pltpu.VMEM)
    return pl.pallas_call(
        merge_kernel,
        in_specs=[whole] * 8,
        out_specs=[whole, whole],
        out_shape=[out, out],
        compiler_params=pltpu.CompilerParams(vmem_limit_bytes=VMEM_LIMIT),
        name="merge_prefix",
    )(*means, *logs)


def final_kernel(where, q_ref, cos_ref, sin_ref, up_ref, mean_ref, log_ref, base_ref, *rest):
    ranks, (kv_out, attention_out, wide) = rest[:4], rest[4:]
    half = q_ref.shape[0]
    start = pl.multiple_of(where[PARITY] * half, half)
    rank = sum(r[...].astype(F32) for r in ranks).astype(BF)
    keys, values = [], []
    for h in range(2):
        for e in range(2):
            delta = jnp.dot(
                rank[:, e * 64 : (e + 1) * 64], up_ref[2 * e + h], preferred_element_type=F32
            )
            part = 2 * h + e
            field = base_ref[:, part * WIDTH : (part + 1) * WIDTH] + delta
            if e == 0:
                field = field * cos_ref[...] + pltpu.roll(field, WIDTH // 2, 1) * sin_ref[...]
            wide[pl.ds(part, NEW_TOK, stride=4), :] = field
            (keys, values)[e].append(field.astype(BF))
    kv_out[...] = wide[pl.ds(start * 4, half * 4), :].astype(BF)
    rows = 8 * half
    token = lax.broadcasted_iota(jnp.int32, (rows, NEW_TOK), 0) % half + start
    seen = lax.broadcasted_iota(jnp.int32, (rows, NEW_TOK), 1) <= token
    ones = jnp.ones((NEW_TOK, WIDTH), BF)
    for h in range(2):
        q = jnp.concatenate(
            [q_ref[:, n * WIDTH : (n + 1) * WIDTH] for n in range(h * 8, h * 8 + 8)], axis=0
        )
        s = lax.dot_general(q, keys[h], (((1,), (1,)), ((), ())), preferred_element_type=F32)
        s = jnp.where(seen, s * SCALE, LOW)
        block = slice(h * rows, (h + 1) * rows)
        log = log_ref[block]
        top = jnp.maximum(log, jnp.max(s, axis=1, keepdims=True))
        weight = jnp.exp2(log - top)
        p = jnp.exp2(s - top).astype(BF)
        value = jnp.dot(
            p, jnp.concatenate([values[h], ones], axis=1), preferred_element_type=F32
        )
        out = (value[:, :WIDTH] + weight * mean_ref[block]) / (value[:, WIDTH:] + weight)
        out = out.astype(BF)
        for j in range(8):
            n = h * 8 + j
            attention_out[:, n * WIDTH : (n + 1) * WIDTH] = out[j * half : (j + 1) * half]


def final(where, queries, cos, sin, up, mean, log, base, ranks):
    half, width = NEW_TOK // 2, queries.shape[1]

    def whole(a):
        return pl.BlockSpec(a.shape, lambda i, w: (0,) * a.ndim)

    rest = [cos, sin, up, mean, log, base, *ranks]
    return pl.pallas_call(
        final_kernel,
        grid_spec=pltpu.PrefetchScalarGridSpec(
            num_scalar_prefetch=1,
            grid=(1,),
            in_specs=[pl.BlockSpec((half, width), lambda i, w: (w[SEQ], 0))]
            + [whole(a) for a in rest],
            out_specs=[
                pl.BlockSpec((half * 4, WIDTH), lambda i, w: (0, 0)),
                pl.BlockSpec((half, width), lambda i, w: (0, 0)),
            ],
            scratch_shapes=[pltpu.VMEM((NEW_TOK * 4, WIDTH), F32)],
        ),
        out_shape=[
            jax.ShapeDtypeStruct((half * 4, WIDTH), BF),
            jax.ShapeDtypeStruct((half, width), BF),
        ],
        compiler_params=pltpu.CompilerParams(vmem_limit_bytes=VMEM_LIMIT),
        name="new_kv_and_attention",
    )(where, queries, *rest)


def rotary_tables():
    exponents = jnp.arange(WIDTH // 2, dtype=F32)
    frequency = jnp.exp(exponents * (-2.0 * math.log(500000.0) / WIDTH))
    positions = CACHE + jnp.arange(NEW_TOK, dtype=jnp.int32)
    angles = positions.astype(F32)[:, None] * frequency[None, :]
    cos, sin = jnp.cos(angles), jnp.sin(angles)
    return jnp.concatenate([cos, cos], axis=1), jnp.concatenate([-sin, sin], axis=1)


def flip(axis, mask):
    return lambda a: lax.ppermute(
        a, axis, [(i, i ^ mask) for i in range(lax.axis_size(axis))]
    )


def shift(axis, step):
    size = lax.axis_size(axis)
    return lambda a: lax.ppermute(a, axis, [(i, (i + step) % size) for i in range(size)])


def local(
    hidden,
    key_value_weight,
    adapter_down_weight,
    adapter_up_weight,
    queries,
    key_value_cache,
    request_adapter,
):
    seq, group, tensor = (lax.axis_index(a) for a in ("seq", "group", "tensor"))
    where = jnp.concatenate(
        [
            jnp.stack([seq, seq // 2, seq % 2, tensor]).astype(jnp.int32),
            lax.dynamic_slice_in_dim(request_adapter, 2 * group, 2),
        ]
    )

    quarter = lax.dynamic_slice(
        adapter_up_weight, (0, seq // 2, 0, seq % 2 * WIDTH), (4, 1, 64, WIDTH)
    )
    maps = jnp.concatenate([adapter_down_weight, quarter[:, 0]], axis=1)
    maps = lax.all_gather(maps, "group", axis=0, tiled=True)

    parts = prep(where, hidden, key_value_weight.reshape(-1, WIDTH))
    base = parts[0].astype(F32)
    for step in (1, 2, 3):
        base += shift("tensor", step)(parts[step]).astype(F32)
    base = base.astype(BF)
    base_own = lax.dynamic_slice_in_dim(base, seq // 2 * NEW_TOK, NEW_TOK, 0)
    base_other = lax.dynamic_slice_in_dim(base, (1 - seq // 2) * NEW_TOK, NEW_TOK, 0)
    base = base_own.astype(F32) + flip("seq", 1)(base_own).astype(F32)
    base += flip("seq", 2)(base_other).astype(F32) + flip("seq", 3)(base_other).astype(F32)

    cache_rows = key_value_cache.reshape(-1, WIDTH)
    o2, o3, l2, l3 = attend(where, queries, cache_rows, True)
    o0, o1, l0, l1 = attend(where, queries, cache_rows, False)
    mean, log = merge(
        [o0, flip("seq", 1)(o1), flip("seq", 2)(o2), flip("seq", 3)(o3)],
        [l0, flip("seq", 1)(l1), flip("seq", 2)(l2), flip("seq", 3)(l3)],
    )
    cos, sin = rotary_tables()

    maps, mean, log, base, cos, sin = lax.optimization_barrier((maps, mean, log, base, cos, sin))

    mine, others = rank_parts(where, hidden, maps)
    rank, up = seq_sum(
        where, mine, [flip("seq", 1)(mine), flip("seq", 2)(others), flip("seq", 3)(others)]
    )
    ranks = [rank] + [shift("tensor", step)(rank) for step in (1, 2, 3)]

    new_kv, attention = final(where, queries, cos, sin, up, mean, log, base, ranks)
    return new_kv.reshape(-1, 2, 2, WIDTH), attention


def solution(mesh):
    in_specs = (
        P("group", ("tensor", "seq")),
        P(("tensor", "seq"), None, None, None),
        P("group", ("tensor", "seq"), None),
        P("group", None, None, "tensor"),
        P("group", "tensor"),
        P("group", "seq", "tensor", None, None),
        P(),
    )
    out_specs = (P(("group", "seq"), "tensor", None, None), P(("group", "seq"), "tensor"))
    return jax.shard_map(local, mesh=mesh, in_specs=in_specs, out_specs=out_specs, check_vma=False)
```

```python
import functools
import math

import jax
import jax.numpy as jnp
from jax import lax
from jax.experimental import pallas as pl
from jax.experimental.pallas import tpu as pltpu
from jax.sharding import PartitionSpec as P

NEW_TOK = 128
CACHE = 16384
WIDTH = 128
SCALE = math.log2(math.e) / math.sqrt(WIDTH)
KEY_BLOCK = 4096
TILE = 256
LOW = -1e30
BF = jnp.bfloat16
F32 = jnp.float32
ATTEND_VMEM = 44 * 2**20
SMALL_VMEM = 16 * 2**20

SEQ, HALF, PARITY, TENSOR, PLANE, CORE, ADAPTERS = 0, 1, 2, 3, 4, 5, 6


def prep_kernel(where, hidden_ref, weight_ref, *rest):
    outs, cols = rest[:4], rest[4]
    depth = hidden_ref.shape[1]
    rows = weight_ref[...].astype(F32).reshape(depth // 8, 8, 2, 8, WIDTH)
    place = lax.broadcasted_iota(jnp.int32, (depth // 8, 8, WIDTH), 1)
    for a in range(2):
        parts = [rows[:, j, a] for j in range(8)]
        for bit in (1, 2, 4):
            odd = (place & bit) != 0
            for j in range(8):
                if not j & bit:
                    low, high = parts[j], parts[j | bit]
                    parts[j] = jnp.where(odd, pltpu.roll(high, bit, 1), low)
                    parts[j | bit] = jnp.where(odd, high, pltpu.roll(low, 8 - bit, 1))
        for c in range(8):
            dest, part = 2 * a + c // 4, c % 4
            cols[dest, :, part * WIDTH : (part + 1) * WIDTH] = (
                parts[c].reshape(depth, WIDTH).astype(BF)
            )
    for step in range(4):
        dest = lax.rem(where[TENSOR] + step, 4)
        outs[step][...] = jnp.dot(
            hidden_ref[...], cols[dest], preferred_element_type=F32
        ).astype(BF)


def prep(where, hidden, weight_rows):
    tokens, depth = hidden.shape
    out = jax.ShapeDtypeStruct((tokens, 4 * WIDTH), BF)
    return pl.pallas_call(
        prep_kernel,
        grid_spec=pltpu.PrefetchScalarGridSpec(
            num_scalar_prefetch=1,
            grid=(1,),
            in_specs=[
                pl.BlockSpec(hidden.shape, lambda i, w: (0, 0)),
                pl.BlockSpec(weight_rows.shape, lambda i, w: (0, 0)),
            ],
            out_specs=[pl.BlockSpec(out.shape, lambda i, w: (0, 0))] * 4,
            scratch_shapes=[pltpu.VMEM((4, depth, 4 * WIDTH), BF)],
        ),
        out_shape=[out] * 4,
        compiler_params=pltpu.CompilerParams(vmem_limit_bytes=SMALL_VMEM),
        cost_estimate=pl.CostEstimate(
            flops=2 * tokens * depth * 16 * WIDTH * 4, bytes_accessed=4 * 2**20, transcendentals=0
        ),
        name="base_partial",
    )(where, hidden, weight_rows)


def attend_kernel(where, q_ref, x_ref, o_first, o_second, acc, top, wide, keys, values):
    block = pl.program_id(0)
    tokens = q_ref.shape[0]
    per_tile = TILE // tokens
    tiles = 8 // per_tile

    @pl.when(block == 0)
    def _():
        acc[...] = jnp.zeros_like(acc)
        top[...] = jnp.full_like(top, LOW)
        for h in range(2):
            values[h, :, WIDTH:] = jnp.ones((KEY_BLOCK, WIDTH), BF)

    wide[...] = x_ref[...].astype(F32)
    for h in range(2):
        keys[h] = wide[pl.ds(2 * h, KEY_BLOCK, stride=4), :].astype(BF)
        values[h, :, :WIDTH] = wide[pl.ds(2 * h + 1, KEY_BLOCK, stride=4), :].astype(BF)

    def score(i):
        h, first = i // tiles, i * per_tile
        q = jnp.concatenate(
            [q_ref[:, (first + j) * WIDTH : (first + j + 1) * WIDTH] for j in range(per_tile)],
            axis=0,
        )
        return lax.dot_general(q, keys[h], (((1,), (1,)), ((), ())), preferred_element_type=F32)

    def absorb(i, s):
        before = top[i]
        after = jnp.maximum(before, jnp.max(s, axis=1, keepdims=True) * SCALE)
        top[i] = after
        fade = jnp.exp2(before - after)
        p = jnp.exp2(s * SCALE - after[:, :1]).astype(BF)
        acc[i] = acc[i] * jnp.concatenate([fade, fade], axis=1) + jnp.dot(
            p, values[i // tiles], preferred_element_type=F32
        )

    ahead = []
    for i in range(0, 2 * tiles, 2):
        now = [(i, score(i)), (i + 1, score(i + 1))]
        for job in ahead:
            absorb(*job)
        ahead = now
    for job in ahead:
        absorb(*job)

    @pl.when(block == pl.num_programs(0) - 1)
    def _():
        half = tokens // 2
        odd = where[PARITY] == 1
        lane = lax.broadcasted_iota(jnp.int32, (tokens, WIDTH), 1)
        logs = jnp.zeros((tokens, WIDTH), F32)
        for h in range(2):
            for t in range(tiles):
                i = h * tiles + t
                total = acc[i, :, WIDTH:]
                mean = (acc[i, :, :WIDTH] / total).astype(BF)
                log = top[i] + jnp.log2(total)
                for j in range(per_tile):
                    n = h * 8 + t * per_tile + j
                    early = mean[j * tokens : j * tokens + half]
                    late = mean[j * tokens + half : (j + 1) * tokens]
                    cols = slice(n * WIDTH, (n + 1) * WIDTH)
                    o_first[:, cols] = jnp.where(odd, late, early)
                    o_second[:, cols] = jnp.where(odd, early, late)
                    logs = jnp.where(lane == n, log[j * tokens : (j + 1) * tokens], logs)
        high = logs.astype(BF).astype(F32)
        middle = (logs - high).astype(BF).astype(F32)
        low = logs - high - middle
        logs = (high + pltpu.roll(middle, 16, 1) + pltpu.roll(low, 32, 1)).astype(BF)
        o_first[:, 16 * WIDTH :] = jnp.where(odd, logs[half:], logs[:half])
        o_second[:, 16 * WIDTH :] = jnp.where(odd, logs[:half], logs[half:])


def attend(where, queries, cache_rows, other):
    tokens, width = NEW_TOK, queries.shape[1]
    blocks = cache_rows.shape[0] // 2 // 4 // KEY_BLOCK
    tiles = 16 * tokens // TILE

    def request(w):
        return 1 - w[HALF] if other else w[HALF]

    o = jax.ShapeDtypeStruct((tokens // 2, width + WIDTH), BF)
    scores = 16 * tokens * blocks * KEY_BLOCK
    return pl.pallas_call(
        attend_kernel,
        grid_spec=pltpu.PrefetchScalarGridSpec(
            num_scalar_prefetch=1,
            grid=(blocks,),
            in_specs=[
                pl.BlockSpec((tokens, width), lambda i, w: (request(w), 0)),
                pl.BlockSpec((KEY_BLOCK * 4, WIDTH), lambda i, w: (request(w) * blocks + i, 0)),
            ],
            out_specs=[pl.BlockSpec(o.shape, lambda i, w: (0, 0))] * 2,
            scratch_shapes=[
                pltpu.VMEM((tiles, TILE, 2 * WIDTH), F32),
                pltpu.VMEM((tiles, TILE, WIDTH), F32),
                pltpu.VMEM((KEY_BLOCK * 4, WIDTH), F32),
                pltpu.VMEM((2, KEY_BLOCK, WIDTH), BF),
                pltpu.VMEM((2, KEY_BLOCK, 2 * WIDTH), BF),
            ],
        ),
        out_shape=[o, o],
        compiler_params=pltpu.CompilerParams(vmem_limit_bytes=ATTEND_VMEM),
        cost_estimate=pl.CostEstimate(
            flops=scores * WIDTH * 8, bytes_accessed=5 * 2**20, transcendentals=scores
        ),
        name="attend_other" if other else "attend_own",
    )(where, queries, cache_rows)


def owner(where, plane, r):
    return where[ADAPTERS + 2 * (2 * plane + where[CORE]) + r]


def when_mine(where, adapter, maps, out, sem):
    down, up, mate_down, mate_up = maps
    mine = adapter // 8 == where[PLANE]
    mates = adapter // 4 % 2 != where[CORE]
    k = adapter % 4
    depth = down.shape[1]
    cols = pl.ds(pl.multiple_of(where[PARITY] * WIDTH, WIDTH), WIDTH)

    def pair(downs, ups):
        return (
            pltpu.make_async_copy(downs.at[k], out.at[:depth], sem.at[0]),
            pltpu.make_async_copy(ups.at[k, where[HALF], :, cols], out.at[depth:], sem.at[1]),
        )

    def start():
        @pl.when(jnp.logical_and(mine, mates))
        def _():
            for copy in pair(mate_down, mate_up):
                copy.start()

        @pl.when(jnp.logical_and(mine, jnp.logical_not(mates)))
        def _():
            for copy in pair(down, up):
                copy.start()

    def wait():
        @pl.when(mine)
        def _():
            for copy in pair(down, up):
                copy.wait()

    return mine, start, wait


def relay_kernel(slots, arrivals, where, *refs):
    maps, came, outs, sem = refs[:4], refs[4 : 4 + arrivals], refs[4 + arrivals : -1], refs[-1]
    waits = []
    for n, (way, slot, hops, r, arrival) in enumerate(slots):
        plane = lax.rem(where[PLANE] + hops + 8, 8)
        out = outs[way].at[slot]
        mine, start, wait = when_mine(where, owner(where, plane, r), maps, out, sem.at[n])
        start()
        waits.append(wait)
        if arrival is not None:

            @pl.when(jnp.logical_not(mine))
            def _(out=out, arrival=arrival):
                out[...] = came[arrival[0]][arrival[1]]

    for wait in waits:
        wait()


def relay(where, maps, came, slots, name):
    height = maps[0].shape[1] + maps[1].shape[2]
    ways = 1 + max(slot[0] for slot in slots)
    outs = [
        jax.ShapeDtypeStruct((sum(slot[0] == way for slot in slots), height, WIDTH), BF)
        for way in range(ways)
    ]
    anywhere = pl.BlockSpec(memory_space=pl.ANY)
    whole = pl.BlockSpec(memory_space=pltpu.VMEM)
    return pl.pallas_call(
        functools.partial(relay_kernel, slots, len(came)),
        in_specs=[pl.BlockSpec(memory_space=pltpu.SMEM)] + [anywhere] * 4 + [whole] * len(came),
        out_specs=[whole] * ways,
        out_shape=outs,
        scratch_shapes=[pltpu.SemaphoreType.DMA((len(slots), 2))],
        compiler_params=pltpu.CompilerParams(vmem_limit_bytes=SMALL_VMEM),
        cost_estimate=pl.CostEstimate(
            flops=0, bytes_accessed=len(slots) * height * 512, transcendentals=0
        ),
        name=name,
    )(where, *maps, *came)


def rank_kernel(where, hidden_ref, base_ref, *refs):
    maps, came, (mine_out, others_out, held, sem) = refs[:4], refs[4:8], refs[8:]
    depth = hidden_ref.shape[1]
    height = held.shape[1] - depth
    waits = []
    for r in range(2):
        adapter = owner(where, where[PLANE], r)
        _, start, wait = when_mine(where, adapter, maps, held.at[r], sem.at[r])
        start()
        waits.append(wait)
        away = lax.rem(where[PLANE] + 8 - adapter // 8, 8)
        odd = away % 2 == 1
        below = away <= 4 if r == 0 else away < 4
        above = jnp.logical_not(below)
        even = jnp.logical_and(away != 0, jnp.logical_not(odd))
        for source, chosen in zip(
            came,
            (
                jnp.logical_and(odd, below),
                jnp.logical_and(even, below),
                jnp.logical_and(odd, above),
                jnp.logical_and(even, above),
            ),
        ):

            @pl.when(chosen)
            def _(r=r, source=source):
                held[r] = source[r]

    half = where[HALF]
    for out, request in ((mine_out, half), (others_out, 1 - half)):
        rows = pl.ds(pl.multiple_of(request * NEW_TOK, NEW_TOK), NEW_TOK)
        for part in range(4):
            start = NEW_TOK + height + part * NEW_TOK
            out[start : start + NEW_TOK] = base_ref[rows, part * WIDTH : (part + 1) * WIDTH]
    for wait in waits:
        wait()
    for out, request in ((mine_out, half), (others_out, 1 - half)):
        rows = pl.ds(pl.multiple_of(request * NEW_TOK, NEW_TOK), NEW_TOK)
        out[:NEW_TOK] = jnp.dot(
            hidden_ref[rows], held[request, :depth], preferred_element_type=F32
        ).astype(BF)
        out[NEW_TOK : NEW_TOK + height] = held[request, depth:]


def rank_parts(where, hidden, base, maps, came):
    height = came[0].shape[1]
    out = jax.ShapeDtypeStruct((5 * NEW_TOK + height - hidden.shape[1], WIDTH), BF)
    anywhere = pl.BlockSpec(memory_space=pl.ANY)
    whole = pl.BlockSpec(memory_space=pltpu.VMEM)
    return pl.pallas_call(
        rank_kernel,
        in_specs=[pl.BlockSpec(memory_space=pltpu.SMEM), whole, whole]
        + [anywhere] * 4
        + [whole] * 4,
        out_specs=[whole, whole],
        out_shape=[out, out],
        scratch_shapes=[pltpu.VMEM((2, height, WIDTH), BF), pltpu.SemaphoreType.DMA((2, 2))],
        compiler_params=pltpu.CompilerParams(vmem_limit_bytes=SMALL_VMEM),
        name="rank_partial",
    )(where, hidden, base, *maps, *came)


def seq_kernel(where, *refs):
    parts, (rank_out, base_out, up_out) = refs[:4], refs[4:]
    after = NEW_TOK + up_out.shape[1]
    rank_out[...] = sum(part[:NEW_TOK].astype(F32) for part in parts).astype(BF)
    for step, part in enumerate(parts):
        up_out[jnp.bitwise_xor(where[SEQ], step)] = part[NEW_TOK:after]
    for col in range(4):
        start = after + col * NEW_TOK
        base_out[:, col * WIDTH : (col + 1) * WIDTH] = sum(
            part[start : start + NEW_TOK].astype(F32) for part in parts
        )


def seq_sum(where, parts):
    whole = pl.BlockSpec(memory_space=pltpu.VMEM)
    return pl.pallas_call(
        seq_kernel,
        in_specs=[pl.BlockSpec(memory_space=pltpu.SMEM)] + [whole] * 4,
        out_specs=[whole] * 3,
        out_shape=[
            jax.ShapeDtypeStruct((NEW_TOK, WIDTH), BF),
            jax.ShapeDtypeStruct((NEW_TOK, 4 * WIDTH), F32),
            jax.ShapeDtypeStruct((4, parts[0].shape[0] - 5 * NEW_TOK, WIDTH), BF),
        ],
        name="seq_sum",
    )(where, *parts)


def merge_kernel(*refs):
    parts, mean_out, log_out = refs[:4], refs[4], refs[5]
    half = parts[0].shape[0]
    tops = []
    for part in parts:
        packed = part[:, 16 * WIDTH :].astype(F32)
        tops.append(packed + pltpu.roll(packed, WIDTH - 16, 1) + pltpu.roll(packed, WIDTH - 32, 1))
    top = functools.reduce(jnp.maximum, tops)
    weights = [jnp.exp2(l - top) for l in tops]
    total = sum(weights)
    merged = top + jnp.log2(total)
    weights = [w / total for w in weights]
    for n in range(16):
        rows = slice(n * half, (n + 1) * half)
        cols = slice(n * WIDTH, (n + 1) * WIDTH)
        mean_out[rows] = sum(
            w[:, n : n + 1] * part[:, cols].astype(F32) for w, part in zip(weights, parts)
        )
        log_out[rows] = jnp.broadcast_to(merged[:, n : n + 1], (half, WIDTH))


def merge(parts):
    out = jax.ShapeDtypeStruct((16 * parts[0].shape[0], WIDTH), F32)
    whole = pl.BlockSpec(memory_space=pltpu.VMEM)
    return pl.pallas_call(
        merge_kernel,
        in_specs=[whole] * 4,
        out_specs=[whole, whole],
        out_shape=[out, out],
        compiler_params=pltpu.CompilerParams(vmem_limit_bytes=SMALL_VMEM),
        name="merge_prefix",
    )(*parts)


def final_kernel(where, q_ref, cos_ref, sin_ref, up_ref, mean_ref, log_ref, base_ref, *rest):
    ranks, (kv_out, attention_out, wide) = rest[:4], rest[4:]
    half = q_ref.shape[0]
    start = pl.multiple_of(where[PARITY] * half, half)
    rank = sum(r[...].astype(F32) for r in ranks).astype(BF)
    keys, values = [], []
    for h in range(2):
        for e in range(2):
            delta = jnp.dot(
                rank[:, e * 64 : (e + 1) * 64], up_ref[2 * e + h], preferred_element_type=F32
            )
            part = 2 * h + e
            field = base_ref[:, part * WIDTH : (part + 1) * WIDTH] + delta
            if e == 0:
                field = field * cos_ref[...] + pltpu.roll(field, WIDTH // 2, 1) * sin_ref[...]
            wide[pl.ds(part, NEW_TOK, stride=4), :] = field
            (keys, values)[e].append(field.astype(BF))
    kv_out[...] = wide[pl.ds(start * 4, half * 4), :].astype(BF)
    rows = 8 * half
    token = lax.broadcasted_iota(jnp.int32, (rows, NEW_TOK), 0) % half + start
    seen = lax.broadcasted_iota(jnp.int32, (rows, NEW_TOK), 1) <= token
    ones = jnp.ones((NEW_TOK, WIDTH), BF)
    for h in range(2):
        q = jnp.concatenate(
            [q_ref[:, n * WIDTH : (n + 1) * WIDTH] for n in range(h * 8, h * 8 + 8)], axis=0
        )
        s = lax.dot_general(q, keys[h], (((1,), (1,)), ((), ())), preferred_element_type=F32)
        s = jnp.where(seen, s * SCALE, LOW)
        block = slice(h * rows, (h + 1) * rows)
        log = log_ref[block]
        top = jnp.maximum(log, jnp.max(s, axis=1, keepdims=True))
        weight = jnp.exp2(log - top)
        p = jnp.exp2(s - top).astype(BF)
        value = jnp.dot(
            p, jnp.concatenate([values[h], ones], axis=1), preferred_element_type=F32
        )
        out = (value[:, :WIDTH] + weight * mean_ref[block]) / (value[:, WIDTH:] + weight)
        out = out.astype(BF)
        for j in range(8):
            n = h * 8 + j
            attention_out[:, n * WIDTH : (n + 1) * WIDTH] = out[j * half : (j + 1) * half]


def final(where, queries, cos, sin, up, mean, log, base, ranks):
    half, width = NEW_TOK // 2, queries.shape[1]

    def whole(a):
        return pl.BlockSpec(a.shape, lambda i, w: (0,) * a.ndim)

    rest = [cos, sin, up, mean, log, base, *ranks]
    return pl.pallas_call(
        final_kernel,
        grid_spec=pltpu.PrefetchScalarGridSpec(
            num_scalar_prefetch=1,
            grid=(1,),
            in_specs=[pl.BlockSpec((half, width), lambda i, w: (w[SEQ], 0))]
            + [whole(a) for a in rest],
            out_specs=[
                pl.BlockSpec((half * 4, WIDTH), lambda i, w: (0, 0)),
                pl.BlockSpec((half, width), lambda i, w: (0, 0)),
            ],
            scratch_shapes=[pltpu.VMEM((NEW_TOK * 4, WIDTH), F32)],
        ),
        out_shape=[
            jax.ShapeDtypeStruct((half * 4, WIDTH), BF),
            jax.ShapeDtypeStruct((half, width), BF),
        ],
        compiler_params=pltpu.CompilerParams(vmem_limit_bytes=SMALL_VMEM),
        name="new_kv_and_attention",
    )(where, queries, *rest)


def rotary_tables():
    exponents = jnp.arange(WIDTH // 2, dtype=F32)
    frequency = jnp.exp(exponents * (-2.0 * math.log(500000.0) / WIDTH))
    positions = CACHE + jnp.arange(NEW_TOK, dtype=jnp.int32)
    angles = positions.astype(F32)[:, None] * frequency[None, :]
    cos, sin = jnp.cos(angles), jnp.sin(angles)
    return jnp.concatenate([cos, cos], axis=1), jnp.concatenate([-sin, sin], axis=1)


def flip(axis, mask):
    return lambda a: lax.ppermute(
        a, axis, [(i, i ^ mask) for i in range(lax.axis_size(axis))]
    )


def shift(axis, step):
    size = lax.axis_size(axis)
    return lambda a: lax.ppermute(a, axis, [(i, (i + step) % size) for i in range(size)])


def tie(value, *others):
    return lax.optimization_barrier((value, *others))[0]


def local(
    hidden,
    key_value_weight,
    adapter_down_weight,
    adapter_up_weight,
    queries,
    key_value_cache,
    request_adapter,
):
    seq, group, tensor = (lax.axis_index(a) for a in ("seq", "group", "tensor"))
    place = jnp.stack([seq, seq // 2, seq % 2, tensor, group // 2, group % 2])
    where = jnp.concatenate([place.astype(jnp.int32), request_adapter])

    maps = [adapter_down_weight, adapter_up_weight]
    maps += [flip("group", 1)(a) for a in maps]

    parts = list(prep(where, hidden, key_value_weight.reshape(-1, WIDTH)))

    far = [(0, 0, 3, 0, None), (0, 1, 3, 1, None), (0, 2, 4, 0, None)]
    far += [(1, 0, -3, 0, None), (1, 1, -3, 1, None), (1, 2, -4, 1, None)]
    near = [(0, 0, 1, 0, (0, 0)), (0, 1, 1, 1, (0, 1)), (1, 0, 2, 0, (0, 2)), (1, 1, 2, 1, None)]
    near += [(2, 0, -1, 0, (1, 0)), (2, 1, -1, 1, (1, 1))]
    near += [(3, 0, -2, 0, None), (3, 1, -2, 1, (1, 2))]

    sent = relay(tie(where, parts[0]), maps, [], far, "relay_far")
    came = [shift("group", 4)(sent[0]), shift("group", -4)(sent[1])]
    parts = list(lax.optimization_barrier((*parts, sent[0]))[:4])
    received = [shift("tensor", step)(parts[step]) for step in (1, 2, 3)]
    cache_rows = key_value_cache.reshape(-1, WIDTH)
    o2, o3 = attend(tie(where, *sent), queries, cache_rows, True)

    sent = relay(tie(where, o2), maps, came, near, "relay_near")
    came = [shift("group", 2 * hops)(a) for hops, a in zip((1, 2, -1, -2), sent)]
    received = lax.optimization_barrier((*received, *sent))[:3]
    base = (parts[0].astype(F32) + sum(r.astype(F32) for r in received)).astype(BF)
    got2 = flip("seq", 2)(tie(o2, *sent))
    o0, o1 = attend(tie(where, *sent, base), queries, cache_rows, False)

    cos, sin = rotary_tables()
    mine, others = rank_parts(tie(where, o1, cos, sin, got2), hidden, base, maps, came)
    rank, base, ups = seq_sum(
        where, [mine, flip("seq", 1)(mine), flip("seq", 2)(others), flip("seq", 3)(others)]
    )
    got1, got3 = flip("seq", 1)(tie(o1, rank)), flip("seq", 3)(tie(o3, rank))
    ranks = [rank] + [shift("tensor", step)(rank) for step in (1, 2, 3)]
    mean, log = merge(list(lax.optimization_barrier((o0, got1, got2, got3, rank)))[:4])

    new_kv, attention = final(where, queries, cos, sin, ups, mean, log, base, ranks)
    return new_kv.reshape(-1, 2, 2, WIDTH), attention


def solution(mesh):
    in_specs = (
        P("group", ("tensor", "seq")),
        P(("tensor", "seq"), None, None, None),
        P("group", ("tensor", "seq"), None),
        P("group", None, None, "tensor"),
        P("group", "tensor"),
        P("group", "seq", "tensor", None, None),
        P(),
    )
    out_specs = (P(("group", "seq"), "tensor", None, None), P(("group", "seq"), "tensor"))
    return jax.shard_map(local, mesh=mesh, in_specs=in_specs, out_specs=out_specs, check_vma=False)
```

```python
import functools
import math

import jax
import jax.numpy as jnp
from jax import lax
from jax.experimental import pallas as pl
from jax.experimental.pallas import tpu as pltpu
from jax.sharding import PartitionSpec as P

NEW_TOK = 128
CACHE = 16384
WIDTH = 128
SCALE = math.log2(math.e) / math.sqrt(WIDTH)
KEY_BLOCK = 4096
TILE = 256
LOW = -1e30
BF = jnp.bfloat16
F32 = jnp.float32
ATTEND_VMEM = 44 * 2**20
SMALL_VMEM = 16 * 2**20

SEQ, HALF, PARITY, TENSOR, PLANE, CORE, ADAPTERS = 0, 1, 2, 3, 4, 5, 6


def prep_kernel(where, hidden_far, weight_far, cache_far, query_far, *rest):
    outs, (cache_out, query_out, hidden_ref, weight_ref, cols, sem) = rest[:4], rest[4:]
    loads = [
        pltpu.make_async_copy(far, near, sem.at[n])
        for n, (far, near) in enumerate(
            (
                (weight_far, weight_ref),
                (hidden_far, hidden_ref),
                (query_far, query_out),
                (cache_far, cache_out),
            )
        )
    ]
    for load in loads:
        load.start()
    for load in loads[:2]:
        load.wait()
    depth = hidden_ref.shape[1]
    rows = weight_ref[...].astype(F32).reshape(depth // 8, 8, 2, 8, WIDTH)
    place = lax.broadcasted_iota(jnp.int32, (depth // 8, 8, WIDTH), 1)
    for a in range(2):
        parts = [rows[:, j, a] for j in range(8)]
        for bit in (1, 2, 4):
            odd = (place & bit) != 0
            for j in range(8):
                if not j & bit:
                    low, high = parts[j], parts[j | bit]
                    parts[j] = jnp.where(odd, pltpu.roll(high, bit, 1), low)
                    parts[j | bit] = jnp.where(odd, high, pltpu.roll(low, 8 - bit, 1))
        for c in range(8):
            dest, part = 2 * a + c // 4, c % 4
            cols[dest, :, part * WIDTH : (part + 1) * WIDTH] = (
                parts[c].reshape(depth, WIDTH).astype(BF)
            )
    for step in range(4):
        dest = lax.rem(where[TENSOR] + step, 4)
        outs[step][...] = jnp.dot(
            hidden_ref[...], cols[dest], preferred_element_type=F32
        ).astype(BF)
    for load in loads[2:]:
        load.wait()


def in_hbm(a):
    return pltpu.with_memory_space_constraint(a, pltpu.HBM)


def prep(where, hidden, weight_rows, cache_rows, queries):
    tokens, depth = hidden.shape
    whole = pl.BlockSpec(memory_space=pltpu.VMEM)
    anywhere = pl.BlockSpec(memory_space=pl.ANY)
    return pl.pallas_call(
        prep_kernel,
        in_specs=[pl.BlockSpec(memory_space=pltpu.SMEM)] + [anywhere] * 4,
        out_specs=[whole] * 6,
        out_shape=[jax.ShapeDtypeStruct((tokens, 4 * WIDTH), BF)] * 4
        + [pltpu.VMEM(cache_rows.shape, BF), pltpu.VMEM(queries.shape, BF)],
        scratch_shapes=[
            pltpu.VMEM(hidden.shape, BF),
            pltpu.VMEM(weight_rows.shape, BF),
            pltpu.VMEM((4, depth, 4 * WIDTH), BF),
            pltpu.SemaphoreType.DMA((4,)),
        ],
        compiler_params=pltpu.CompilerParams(vmem_limit_bytes=SMALL_VMEM),
        cost_estimate=pl.CostEstimate(
            flops=2 * tokens * depth * 16 * WIDTH, bytes_accessed=11 * 2**20, transcendentals=0
        ),
        name="base_partial",
    )(where, *map(in_hbm, (hidden, weight_rows, cache_rows, queries)))


def attend_kernel(where, q_ref, x_ref, o_first, o_second, acc, top, wide, keys, values):
    block = pl.program_id(0)
    tokens = q_ref.shape[0]
    per_tile = TILE // tokens
    tiles = 8 // per_tile

    @pl.when(block == 0)
    def _():
        acc[...] = jnp.zeros_like(acc)
        top[...] = jnp.full_like(top, LOW)
        for h in range(2):
            values[h, :, WIDTH:] = jnp.ones((KEY_BLOCK, WIDTH), BF)

    wide[...] = x_ref[...].astype(F32)
    for h in range(2):
        keys[h] = wide[pl.ds(2 * h, KEY_BLOCK, stride=4), :].astype(BF)
        values[h, :, :WIDTH] = wide[pl.ds(2 * h + 1, KEY_BLOCK, stride=4), :].astype(BF)

    def score(i):
        h, first = i // tiles, i * per_tile
        q = jnp.concatenate(
            [q_ref[:, (first + j) * WIDTH : (first + j + 1) * WIDTH] for j in range(per_tile)],
            axis=0,
        )
        return lax.dot_general(q, keys[h], (((1,), (1,)), ((), ())), preferred_element_type=F32)

    def absorb(i, s):
        before = top[i]
        after = jnp.maximum(before, jnp.max(s, axis=1, keepdims=True) * SCALE)
        top[i] = after
        fade = jnp.exp2(before - after)
        p = jnp.exp2(s * SCALE - after[:, :1]).astype(BF)
        acc[i] = acc[i] * jnp.concatenate([fade, fade], axis=1) + jnp.dot(
            p, values[i // tiles], preferred_element_type=F32
        )

    ahead = []
    for i in range(0, 2 * tiles, 2):
        now = [(i, score(i)), (i + 1, score(i + 1))]
        for job in ahead:
            absorb(*job)
        ahead = now
    for job in ahead:
        absorb(*job)

    @pl.when(block == pl.num_programs(0) - 1)
    def _():
        half = tokens // 2
        odd = where[PARITY] == 1
        lane = lax.broadcasted_iota(jnp.int32, (tokens, WIDTH), 1)
        logs = jnp.zeros((tokens, WIDTH), F32)
        for h in range(2):
            for t in range(tiles):
                i = h * tiles + t
                total = acc[i, :, WIDTH:]
                mean = (acc[i, :, :WIDTH] / total).astype(BF)
                log = top[i] + jnp.log2(total)
                for j in range(per_tile):
                    n = h * 8 + t * per_tile + j
                    early = mean[j * tokens : j * tokens + half]
                    late = mean[j * tokens + half : (j + 1) * tokens]
                    cols = slice(n * WIDTH, (n + 1) * WIDTH)
                    o_first[:, cols] = jnp.where(odd, late, early)
                    o_second[:, cols] = jnp.where(odd, early, late)
                    logs = jnp.where(lane == n, log[j * tokens : (j + 1) * tokens], logs)
        high = logs.astype(BF).astype(F32)
        middle = (logs - high).astype(BF).astype(F32)
        low = logs - high - middle
        logs = (high + pltpu.roll(middle, 16, 1) + pltpu.roll(low, 32, 1)).astype(BF)
        o_first[:, 16 * WIDTH :] = jnp.where(odd, logs[half:], logs[:half])
        o_second[:, 16 * WIDTH :] = jnp.where(odd, logs[:half], logs[half:])


def attend(where, queries, cache_rows, other):
    tokens, width = NEW_TOK, queries.shape[1]
    blocks = cache_rows.shape[0] // 2 // 4 // KEY_BLOCK
    tiles = 16 * tokens // TILE

    def request(w):
        return 1 - w[HALF] if other else w[HALF]

    o = jax.ShapeDtypeStruct((tokens // 2, width + WIDTH), BF)
    scores = 16 * tokens * blocks * KEY_BLOCK
    return pl.pallas_call(
        attend_kernel,
        grid_spec=pltpu.PrefetchScalarGridSpec(
            num_scalar_prefetch=1,
            grid=(blocks,),
            in_specs=[
                pl.BlockSpec((tokens, width), lambda i, w: (request(w), 0)),
                pl.BlockSpec((KEY_BLOCK * 4, WIDTH), lambda i, w: (request(w) * blocks + i, 0)),
            ],
            out_specs=[pl.BlockSpec(o.shape, lambda i, w: (0, 0))] * 2,
            scratch_shapes=[
                pltpu.VMEM((tiles, TILE, 2 * WIDTH), F32),
                pltpu.VMEM((tiles, TILE, WIDTH), F32),
                pltpu.VMEM((KEY_BLOCK * 4, WIDTH), F32),
                pltpu.VMEM((2, KEY_BLOCK, WIDTH), BF),
                pltpu.VMEM((2, KEY_BLOCK, 2 * WIDTH), BF),
            ],
        ),
        out_shape=[o, o],
        compiler_params=pltpu.CompilerParams(vmem_limit_bytes=ATTEND_VMEM),
        cost_estimate=pl.CostEstimate(
            flops=scores * WIDTH * 8, bytes_accessed=5 * 2**20, transcendentals=scores
        ),
        name="attend_other" if other else "attend_own",
    )(where, queries, cache_rows)


def owner(where, plane, r):
    return where[ADAPTERS + 2 * (2 * plane + where[CORE]) + r]


def when_mine(where, adapter, maps, out, sem):
    down, up, mate_down, mate_up = maps
    mine = adapter // 8 == where[PLANE]
    mates = adapter // 4 % 2 != where[CORE]
    k = adapter % 4
    depth = down.shape[1]
    cols = pl.ds(pl.multiple_of(where[PARITY] * WIDTH, WIDTH), WIDTH)

    def pair(downs, ups):
        return (
            pltpu.make_async_copy(downs.at[k], out.at[:depth], sem.at[0]),
            pltpu.make_async_copy(ups.at[k, where[HALF], :, cols], out.at[depth:], sem.at[1]),
        )

    def start():
        @pl.when(jnp.logical_and(mine, mates))
        def _():
            for copy in pair(mate_down, mate_up):
                copy.start()

        @pl.when(jnp.logical_and(mine, jnp.logical_not(mates)))
        def _():
            for copy in pair(down, up):
                copy.start()

    def wait():
        @pl.when(mine)
        def _():
            for copy in pair(down, up):
                copy.wait()

    return mine, start, wait


def relay_kernel(slots, arrivals, where, *refs):
    maps, came, outs, sem = refs[:4], refs[4 : 4 + arrivals], refs[4 + arrivals : -1], refs[-1]
    waits = []
    for n, (way, slot, hops, r, arrival) in enumerate(slots):
        plane = lax.rem(where[PLANE] + hops + 8, 8)
        out = outs[way].at[slot]
        mine, start, wait = when_mine(where, owner(where, plane, r), maps, out, sem.at[n])
        start()
        waits.append(wait)
        if arrival is not None:

            @pl.when(jnp.logical_not(mine))
            def _(out=out, arrival=arrival):
                out[...] = came[arrival[0]][arrival[1]]

    for wait in waits:
        wait()


def relay(where, maps, came, slots, name):
    height = maps[0].shape[1] + maps[1].shape[2]
    ways = 1 + max(slot[0] for slot in slots)
    outs = [
        jax.ShapeDtypeStruct((sum(slot[0] == way for slot in slots), height, WIDTH), BF)
        for way in range(ways)
    ]
    anywhere = pl.BlockSpec(memory_space=pl.ANY)
    whole = pl.BlockSpec(memory_space=pltpu.VMEM)
    return pl.pallas_call(
        functools.partial(relay_kernel, slots, len(came)),
        in_specs=[pl.BlockSpec(memory_space=pltpu.SMEM)] + [anywhere] * 4 + [whole] * len(came),
        out_specs=[whole] * ways,
        out_shape=outs,
        scratch_shapes=[pltpu.SemaphoreType.DMA((len(slots), 2))],
        compiler_params=pltpu.CompilerParams(vmem_limit_bytes=SMALL_VMEM),
        cost_estimate=pl.CostEstimate(
            flops=0, bytes_accessed=2 * 2**20, transcendentals=0
        ),
        name=name,
    )(where, *map(in_hbm, maps[:2]), *maps[2:], *came)


def rank_kernel(where, hidden_ref, base_ref, *refs):
    maps, came, (mine_out, others_out, held, sem) = refs[:4], refs[4:8], refs[8:]
    depth = hidden_ref.shape[1]
    height = held.shape[1] - depth
    waits = []
    for r in range(2):
        adapter = owner(where, where[PLANE], r)
        _, start, wait = when_mine(where, adapter, maps, held.at[r], sem.at[r])
        start()
        waits.append(wait)
        away = lax.rem(where[PLANE] + 8 - adapter // 8, 8)
        odd = away % 2 == 1
        below = away <= 4 if r == 0 else away < 4
        above = jnp.logical_not(below)
        even = jnp.logical_and(away != 0, jnp.logical_not(odd))
        for source, chosen in zip(
            came,
            (
                jnp.logical_and(odd, below),
                jnp.logical_and(even, below),
                jnp.logical_and(odd, above),
                jnp.logical_and(even, above),
            ),
        ):

            @pl.when(chosen)
            def _(r=r, source=source):
                held[r] = source[r]

    half = where[HALF]
    for out, request in ((mine_out, half), (others_out, 1 - half)):
        rows = pl.ds(pl.multiple_of(request * NEW_TOK, NEW_TOK), NEW_TOK)
        for part in range(4):
            start = NEW_TOK + height + part * NEW_TOK
            out[start : start + NEW_TOK] = base_ref[rows, part * WIDTH : (part + 1) * WIDTH]
    for wait in waits:
        wait()
    for out, request in ((mine_out, half), (others_out, 1 - half)):
        rows = pl.ds(pl.multiple_of(request * NEW_TOK, NEW_TOK), NEW_TOK)
        out[:NEW_TOK] = jnp.dot(
            hidden_ref[rows], held[request, :depth], preferred_element_type=F32
        ).astype(BF)
        out[NEW_TOK : NEW_TOK + height] = held[request, depth:]


def rank_parts(where, hidden, base, maps, came):
    height = came[0].shape[1]
    out = jax.ShapeDtypeStruct((5 * NEW_TOK + height - hidden.shape[1], WIDTH), BF)
    anywhere = pl.BlockSpec(memory_space=pl.ANY)
    whole = pl.BlockSpec(memory_space=pltpu.VMEM)
    return pl.pallas_call(
        rank_kernel,
        in_specs=[pl.BlockSpec(memory_space=pltpu.SMEM), whole, whole]
        + [anywhere] * 4
        + [whole] * 4,
        out_specs=[whole, whole],
        out_shape=[out, out],
        scratch_shapes=[pltpu.VMEM((2, height, WIDTH), BF), pltpu.SemaphoreType.DMA((2, 2))],
        compiler_params=pltpu.CompilerParams(vmem_limit_bytes=SMALL_VMEM),
        name="rank_partial",
    )(where, hidden, base, *map(in_hbm, maps[:2]), *maps[2:], *came)


def seq_kernel(where, *refs):
    parts, (rank_out, base_out, up_out) = refs[:4], refs[4:]
    after = NEW_TOK + up_out.shape[1]
    rank_out[...] = sum(part[:NEW_TOK].astype(F32) for part in parts).astype(BF)
    for step, part in enumerate(parts):
        up_out[jnp.bitwise_xor(where[SEQ], step)] = part[NEW_TOK:after]
    for col in range(4):
        start = after + col * NEW_TOK
        base_out[:, col * WIDTH : (col + 1) * WIDTH] = sum(
            part[start : start + NEW_TOK].astype(F32) for part in parts
        )


def seq_sum(where, parts):
    whole = pl.BlockSpec(memory_space=pltpu.VMEM)
    return pl.pallas_call(
        seq_kernel,
        in_specs=[pl.BlockSpec(memory_space=pltpu.SMEM)] + [whole] * 4,
        out_specs=[whole] * 3,
        out_shape=[
            jax.ShapeDtypeStruct((NEW_TOK, WIDTH), BF),
            jax.ShapeDtypeStruct((NEW_TOK, 4 * WIDTH), F32),
            jax.ShapeDtypeStruct((4, parts[0].shape[0] - 5 * NEW_TOK, WIDTH), BF),
        ],
        compiler_params=pltpu.CompilerParams(vmem_limit_bytes=SMALL_VMEM),
        name="seq_sum",
    )(where, *parts)


def merge_kernel(*refs):
    parts, mean_out, log_out = refs[:4], refs[4], refs[5]
    half = parts[0].shape[0]
    tops = []
    for part in parts:
        packed = part[:, 16 * WIDTH :].astype(F32)
        tops.append(packed + pltpu.roll(packed, WIDTH - 16, 1) + pltpu.roll(packed, WIDTH - 32, 1))
    top = functools.reduce(jnp.maximum, tops)
    weights = [jnp.exp2(l - top) for l in tops]
    total = sum(weights)
    merged = top + jnp.log2(total)
    weights = [w / total for w in weights]
    for n in range(16):
        rows = slice(n * half, (n + 1) * half)
        cols = slice(n * WIDTH, (n + 1) * WIDTH)
        mean_out[rows] = sum(
            w[:, n : n + 1] * part[:, cols].astype(F32) for w, part in zip(weights, parts)
        )
        log_out[rows] = jnp.broadcast_to(merged[:, n : n + 1], (half, WIDTH))


def merge(parts):
    out = jax.ShapeDtypeStruct((16 * parts[0].shape[0], WIDTH), F32)
    whole = pl.BlockSpec(memory_space=pltpu.VMEM)
    return pl.pallas_call(
        merge_kernel,
        in_specs=[whole] * 4,
        out_specs=[whole, whole],
        out_shape=[out, out],
        compiler_params=pltpu.CompilerParams(vmem_limit_bytes=SMALL_VMEM),
        name="merge_prefix",
    )(*parts)


def final_kernel(where, q_ref, cos_ref, sin_ref, up_ref, mean_ref, log_ref, base_ref, *rest):
    ranks, (kv_out, attention_out, wide) = rest[:4], rest[4:]
    half = q_ref.shape[0]
    start = pl.multiple_of(where[PARITY] * half, half)
    rank = sum(r[...].astype(F32) for r in ranks).astype(BF)
    keys, values = [], []
    for h in range(2):
        for e in range(2):
            delta = jnp.dot(
                rank[:, e * 64 : (e + 1) * 64], up_ref[2 * e + h], preferred_element_type=F32
            )
            part = 2 * h + e
            field = base_ref[:, part * WIDTH : (part + 1) * WIDTH] + delta
            if e == 0:
                field = field * cos_ref[...] + pltpu.roll(field, WIDTH // 2, 1) * sin_ref[...]
            wide[pl.ds(part, NEW_TOK, stride=4), :] = field
            (keys, values)[e].append(field.astype(BF))
    kv_out[...] = wide[pl.ds(start * 4, half * 4), :].astype(BF)
    rows = 8 * half
    token = lax.broadcasted_iota(jnp.int32, (rows, NEW_TOK), 0) % half + start
    seen = lax.broadcasted_iota(jnp.int32, (rows, NEW_TOK), 1) <= token
    ones = jnp.ones((NEW_TOK, WIDTH), BF)
    for h in range(2):
        q = jnp.concatenate(
            [q_ref[:, n * WIDTH : (n + 1) * WIDTH] for n in range(h * 8, h * 8 + 8)], axis=0
        )
        s = lax.dot_general(q, keys[h], (((1,), (1,)), ((), ())), preferred_element_type=F32)
        s = jnp.where(seen, s * SCALE, LOW)
        block = slice(h * rows, (h + 1) * rows)
        log = log_ref[block]
        top = jnp.maximum(log, jnp.max(s, axis=1, keepdims=True))
        weight = jnp.exp2(log - top)
        p = jnp.exp2(s - top).astype(BF)
        value = jnp.dot(
            p, jnp.concatenate([values[h], ones], axis=1), preferred_element_type=F32
        )
        out = (value[:, :WIDTH] + weight * mean_ref[block]) / (value[:, WIDTH:] + weight)
        out = out.astype(BF)
        for j in range(8):
            n = h * 8 + j
            attention_out[:, n * WIDTH : (n + 1) * WIDTH] = out[j * half : (j + 1) * half]


def final(where, queries, cos, sin, up, mean, log, base, ranks):
    half, width = NEW_TOK // 2, queries.shape[1]

    def whole(a):
        return pl.BlockSpec(a.shape, lambda i, w: (0,) * a.ndim)

    rest = [cos, sin, up, mean, log, base, *ranks]
    return pl.pallas_call(
        final_kernel,
        grid_spec=pltpu.PrefetchScalarGridSpec(
            num_scalar_prefetch=1,
            grid=(1,),
            in_specs=[pl.BlockSpec((half, width), lambda i, w: (w[SEQ], 0))]
            + [whole(a) for a in rest],
            out_specs=[
                pl.BlockSpec((half * 4, WIDTH), lambda i, w: (0, 0)),
                pl.BlockSpec((half, width), lambda i, w: (0, 0)),
            ],
            scratch_shapes=[pltpu.VMEM((NEW_TOK * 4, WIDTH), F32)],
        ),
        out_shape=[
            jax.ShapeDtypeStruct((half * 4, WIDTH), BF),
            jax.ShapeDtypeStruct((half, width), BF),
        ],
        compiler_params=pltpu.CompilerParams(vmem_limit_bytes=SMALL_VMEM),
        name="new_kv_and_attention",
    )(where, queries, *rest)


def rotary_tables():
    exponents = jnp.arange(WIDTH // 2, dtype=F32)
    frequency = jnp.exp(exponents * (-2.0 * math.log(500000.0) / WIDTH))
    positions = CACHE + jnp.arange(NEW_TOK, dtype=jnp.int32)
    angles = positions.astype(F32)[:, None] * frequency[None, :]
    cos, sin = jnp.cos(angles), jnp.sin(angles)
    return jnp.concatenate([cos, cos], axis=1), jnp.concatenate([-sin, sin], axis=1)


def flip(axis, mask):
    return lambda a: lax.ppermute(
        a, axis, [(i, i ^ mask) for i in range(lax.axis_size(axis))]
    )


def shift(axis, step):
    size = lax.axis_size(axis)
    return lambda a: lax.ppermute(a, axis, [(i, (i + step) % size) for i in range(size)])


def tie(value, *others):
    return lax.optimization_barrier((value, *others))[0]


def local(
    hidden,
    key_value_weight,
    adapter_down_weight,
    adapter_up_weight,
    queries,
    key_value_cache,
    request_adapter,
):
    seq, group, tensor = (lax.axis_index(a) for a in ("seq", "group", "tensor"))
    place = jnp.stack([seq, seq // 2, seq % 2, tensor, group // 2, group % 2])
    where = jnp.concatenate([place.astype(jnp.int32), request_adapter])

    maps = [adapter_down_weight, adapter_up_weight]
    maps += [flip("group", 1)(a) for a in maps]

    far = [(0, 0, 3, 0, None), (0, 1, 3, 1, None), (0, 2, 4, 0, None)]
    far += [(1, 0, -3, 0, None), (1, 1, -3, 1, None), (1, 2, -4, 1, None)]
    near = [(0, 0, 1, 0, (0, 0)), (0, 1, 1, 1, (0, 1)), (1, 0, 2, 0, (0, 2)), (1, 1, 2, 1, None)]
    near += [(2, 0, -1, 0, (1, 0)), (2, 1, -1, 1, (1, 1))]
    near += [(3, 0, -2, 0, None), (3, 1, -2, 1, (1, 2))]

    sent = relay(where, maps, [], far, "relay_far")
    came = [shift("group", 4)(sent[0]), shift("group", -4)(sent[1])]

    cache_rows = key_value_cache.reshape(-1, WIDTH)
    *parts, cache_rows, queries = prep(
        tie(where, *sent), hidden, key_value_weight.reshape(-1, WIDTH), cache_rows, queries
    )
    received = [shift("tensor", step)(parts[step]) for step in (1, 2, 3)]
    o2, o3 = attend(tie(where, parts[0]), queries, cache_rows, True)

    sent = relay(tie(where, o2), maps, came, near, "relay_near")
    came = [shift("group", 2 * hops)(a) for hops, a in zip((1, 2, -1, -2), sent)]
    received = lax.optimization_barrier((*received, *sent))[:3]
    base = (parts[0].astype(F32) + sum(r.astype(F32) for r in received)).astype(BF)
    got2 = flip("seq", 2)(tie(o2, *sent))
    o0, o1 = attend(tie(where, *sent, base), queries, cache_rows, False)

    cos, sin = rotary_tables()
    mine, others = rank_parts(tie(where, o1, cos, sin, got2), hidden, base, maps, came)
    rank, base, ups = seq_sum(
        where, [mine, flip("seq", 1)(mine), flip("seq", 2)(others), flip("seq", 3)(others)]
    )
    got1, got3 = flip("seq", 1)(tie(o1, rank)), flip("seq", 3)(tie(o3, rank))
    ranks = [rank] + [shift("tensor", step)(rank) for step in (1, 2, 3)]
    mean, log = merge(list(lax.optimization_barrier((o0, got1, got2, got3, rank)))[:4])

    new_kv, attention = final(where, queries, cos, sin, ups, mean, log, base, ranks)
    return new_kv.reshape(-1, 2, 2, WIDTH), attention


def solution(mesh):
    in_specs = (
        P("group", ("tensor", "seq")),
        P(("tensor", "seq"), None, None, None),
        P("group", ("tensor", "seq"), None),
        P("group", None, None, "tensor"),
        P("group", "tensor"),
        P("group", "seq", "tensor", None, None),
        P(),
    )
    out_specs = (P(("group", "seq"), "tensor", None, None), P(("group", "seq"), "tensor"))
    return jax.shard_map(local, mesh=mesh, in_specs=in_specs, out_specs=out_specs, check_vma=False)
```

```python
import functools
import math

import jax
import jax.numpy as jnp
from jax import lax
from jax.experimental import pallas as pl
from jax.experimental.pallas import tpu as pltpu
from jax.sharding import PartitionSpec as P

NEW_TOK = 128
CACHE = 16384
WIDTH = 128
SCALE = math.log2(math.e) / math.sqrt(WIDTH)
KEY_BLOCK = 4096
BODY = 4
TILE = 256
LOW = -1e30
BF = jnp.bfloat16
F32 = jnp.float32
ATTEND_VMEM = 44 * 2**20
SMALL_VMEM = 16 * 2**20

SEQ, HALF, PARITY, TENSOR, PLANE, CORE, ADAPTERS = 0, 1, 2, 3, 4, 5, 6


def prep_kernel(where, hidden_far, weight_far, cache_far, query_far, *rest):
    outs, (cache_out, query_out, hidden_ref, weight_ref, cols, sem) = rest[:4], rest[4:]
    loads = [
        pltpu.make_async_copy(far, near, sem.at[n])
        for n, (far, near) in enumerate(
            (
                (weight_far, weight_ref),
                (hidden_far, hidden_ref),
                (query_far, query_out),
                (cache_far, cache_out),
            )
        )
    ]
    for load in loads:
        load.start()
    for load in loads[:2]:
        load.wait()
    depth = hidden_ref.shape[1]
    rows = weight_ref[...].astype(F32).reshape(depth // 8, 8, 2, 8, WIDTH)
    place = lax.broadcasted_iota(jnp.int32, (depth // 8, 8, WIDTH), 1)
    for a in range(2):
        parts = [rows[:, j, a] for j in range(8)]
        for bit in (1, 2, 4):
            odd = (place & bit) != 0
            for j in range(8):
                if not j & bit:
                    low, high = parts[j], parts[j | bit]
                    parts[j] = jnp.where(odd, pltpu.roll(high, bit, 1), low)
                    parts[j | bit] = jnp.where(odd, high, pltpu.roll(low, 8 - bit, 1))
        for c in range(8):
            dest, part = 2 * a + c // 4, c % 4
            cols[dest, :, part * WIDTH : (part + 1) * WIDTH] = (
                parts[c].reshape(depth, WIDTH).astype(BF)
            )
    for step in range(4):
        dest = lax.rem(where[TENSOR] + step, 4)
        outs[step][...] = jnp.dot(
            hidden_ref[...], cols[dest], preferred_element_type=F32
        ).astype(BF)
    for load in loads[2:]:
        load.wait()


def in_hbm(a):
    return pltpu.with_memory_space_constraint(a, pltpu.HBM)


def prep(where, hidden, weight_rows, cache_rows, queries):
    tokens, depth = hidden.shape
    whole = pl.BlockSpec(memory_space=pltpu.VMEM)
    anywhere = pl.BlockSpec(memory_space=pl.ANY)
    return pl.pallas_call(
        prep_kernel,
        in_specs=[pl.BlockSpec(memory_space=pltpu.SMEM)] + [anywhere] * 4,
        out_specs=[whole] * 6,
        out_shape=[jax.ShapeDtypeStruct((tokens, 4 * WIDTH), BF)] * 4
        + [pltpu.VMEM(cache_rows.shape, BF), pltpu.VMEM(queries.shape, BF)],
        scratch_shapes=[
            pltpu.VMEM(hidden.shape, BF),
            pltpu.VMEM(weight_rows.shape, BF),
            pltpu.VMEM((4, depth, 4 * WIDTH), BF),
            pltpu.SemaphoreType.DMA((4,)),
        ],
        compiler_params=pltpu.CompilerParams(vmem_limit_bytes=SMALL_VMEM),
        cost_estimate=pl.CostEstimate(
            flops=2 * tokens * depth * 16 * WIDTH, bytes_accessed=11 * 2**20, transcendentals=0
        ),
        name="base_partial",
    )(where, *map(in_hbm, (hidden, weight_rows, cache_rows, queries)))


def attend_kernel(where, q_ref, x_ref, o_first, o_second, acc, top, wide, keys, values):
    block = pl.program_id(0)
    tokens = q_ref.shape[0]
    per_tile = TILE // tokens
    tiles = 8 // per_tile

    @pl.when(block == 0)
    def _():
        acc[...] = jnp.zeros_like(acc)
        top[...] = jnp.full_like(top, LOW)
        for h in range(2):
            values[h, :, WIDTH:] = jnp.ones((KEY_BLOCK, WIDTH), BF)

    wide[...] = x_ref[...].astype(F32)
    for h in range(2):
        keys[h] = wide[pl.ds(2 * h, KEY_BLOCK, stride=4), :].astype(BF)
        values[h, :, :WIDTH] = wide[pl.ds(2 * h + 1, KEY_BLOCK, stride=4), :].astype(BF)

    def score(h, t):
        first = h * 8 + t * per_tile
        q = jnp.concatenate(
            [
                q_ref[:, pl.ds(pl.multiple_of((first + j) * WIDTH, WIDTH), WIDTH)]
                for j in range(per_tile)
            ],
            axis=0,
        )
        return lax.dot_general(q, keys[h], (((1,), (1,)), ((), ())), preferred_element_type=F32)

    def absorb(h, t, s):
        i = h * tiles + t
        before = top[i]
        after = jnp.maximum(before, jnp.max(s, axis=1, keepdims=True) * SCALE)
        top[i] = after
        fade = jnp.exp2(before - after)
        p = jnp.exp2(s * SCALE - after[:, :1]).astype(BF)
        acc[i] = acc[i] * jnp.concatenate([fade, fade], axis=1) + jnp.dot(
            p, values[h], preferred_element_type=F32
        )

    def turn(k, _):
        h, start = k // (tiles // BODY), k % (tiles // BODY) * BODY
        ahead = []
        for t in range(0, BODY, 2):
            now = [(start + u, score(h, start + u)) for u in (t, t + 1)]
            for job in ahead:
                absorb(h, *job)
            ahead = now
        for job in ahead:
            absorb(h, *job)
        return 0

    lax.fori_loop(0, 2 * tiles // BODY, turn, 0)

    @pl.when(block == pl.num_programs(0) - 1)
    def _():
        half = tokens // 2
        odd = where[PARITY] == 1
        lane = lax.broadcasted_iota(jnp.int32, (tokens, WIDTH), 1)
        logs = jnp.zeros((tokens, WIDTH), F32)
        for h in range(2):
            for t in range(tiles):
                i = h * tiles + t
                total = acc[i, :, WIDTH:]
                mean = (acc[i, :, :WIDTH] / total).astype(BF)
                log = top[i] + jnp.log2(total)
                for j in range(per_tile):
                    n = h * 8 + t * per_tile + j
                    early = mean[j * tokens : j * tokens + half]
                    late = mean[j * tokens + half : (j + 1) * tokens]
                    cols = slice(n * WIDTH, (n + 1) * WIDTH)
                    o_first[:, cols] = jnp.where(odd, late, early)
                    o_second[:, cols] = jnp.where(odd, early, late)
                    logs = jnp.where(lane == n, log[j * tokens : (j + 1) * tokens], logs)
        high = logs.astype(BF).astype(F32)
        middle = (logs - high).astype(BF).astype(F32)
        low = logs - high - middle
        logs = (high + pltpu.roll(middle, 16, 1) + pltpu.roll(low, 32, 1)).astype(BF)
        o_first[:, 16 * WIDTH :] = jnp.where(odd, logs[half:], logs[:half])
        o_second[:, 16 * WIDTH :] = jnp.where(odd, logs[:half], logs[half:])


def attend(where, queries, cache_rows, other):
    tokens, width = NEW_TOK, queries.shape[1]
    blocks = cache_rows.shape[0] // 2 // 4 // KEY_BLOCK
    tiles = 16 * tokens // TILE

    def request(w):
        return 1 - w[HALF] if other else w[HALF]

    o = jax.ShapeDtypeStruct((tokens // 2, width + WIDTH), BF)
    scores = 16 * tokens * blocks * KEY_BLOCK
    return pl.pallas_call(
        attend_kernel,
        grid_spec=pltpu.PrefetchScalarGridSpec(
            num_scalar_prefetch=1,
            grid=(blocks,),
            in_specs=[
                pl.BlockSpec((tokens, width), lambda i, w: (request(w), 0)),
                pl.BlockSpec((KEY_BLOCK * 4, WIDTH), lambda i, w: (request(w) * blocks + i, 0)),
            ],
            out_specs=[pl.BlockSpec(o.shape, lambda i, w: (0, 0))] * 2,
            scratch_shapes=[
                pltpu.VMEM((tiles, TILE, 2 * WIDTH), F32),
                pltpu.VMEM((tiles, TILE, WIDTH), F32),
                pltpu.VMEM((KEY_BLOCK * 4, WIDTH), F32),
                pltpu.VMEM((2, KEY_BLOCK, WIDTH), BF),
                pltpu.VMEM((2, KEY_BLOCK, 2 * WIDTH), BF),
            ],
        ),
        out_shape=[o, o],
        compiler_params=pltpu.CompilerParams(vmem_limit_bytes=ATTEND_VMEM),
        cost_estimate=pl.CostEstimate(
            flops=scores * WIDTH * 8, bytes_accessed=5 * 2**20, transcendentals=scores
        ),
        name="attend_other" if other else "attend_own",
    )(where, queries, cache_rows)


def owner(where, plane, r):
    return where[ADAPTERS + 2 * (2 * plane + where[CORE]) + r]


def when_mine(where, adapter, maps, out, sem):
    down, up, mate_down, mate_up = maps
    mine = adapter // 8 == where[PLANE]
    mates = adapter // 4 % 2 != where[CORE]
    k = adapter % 4
    depth = down.shape[1]
    cols = pl.ds(pl.multiple_of(where[PARITY] * WIDTH, WIDTH), WIDTH)

    def pair(downs, ups):
        return (
            pltpu.make_async_copy(downs.at[k], out.at[:depth], sem.at[0]),
            pltpu.make_async_copy(ups.at[k, where[HALF], :, cols], out.at[depth:], sem.at[1]),
        )

    def start():
        @pl.when(jnp.logical_and(mine, mates))
        def _():
            for copy in pair(mate_down, mate_up):
                copy.start()

        @pl.when(jnp.logical_and(mine, jnp.logical_not(mates)))
        def _():
            for copy in pair(down, up):
                copy.start()

    def wait():
        @pl.when(mine)
        def _():
            for copy in pair(down, up):
                copy.wait()

    return mine, start, wait


def relay_kernel(slots, arrivals, where, *refs):
    maps, came, outs, sem = refs[:4], refs[4 : 4 + arrivals], refs[4 + arrivals : -1], refs[-1]
    waits = []
    for n, (way, slot, hops, r, arrival) in enumerate(slots):
        plane = lax.rem(where[PLANE] + hops + 8, 8)
        out = outs[way].at[slot]
        mine, start, wait = when_mine(where, owner(where, plane, r), maps, out, sem.at[n])
        start()
        waits.append(wait)
        if arrival is not None:

            @pl.when(jnp.logical_not(mine))
            def _(out=out, arrival=arrival):
                out[...] = came[arrival[0]][arrival[1]]

    for wait in waits:
        wait()


def relay(where, maps, came, slots, name):
    height = maps[0].shape[1] + maps[1].shape[2]
    ways = 1 + max(slot[0] for slot in slots)
    outs = [
        jax.ShapeDtypeStruct((sum(slot[0] == way for slot in slots), height, WIDTH), BF)
        for way in range(ways)
    ]
    anywhere = pl.BlockSpec(memory_space=pl.ANY)
    whole = pl.BlockSpec(memory_space=pltpu.VMEM)
    return pl.pallas_call(
        functools.partial(relay_kernel, slots, len(came)),
        in_specs=[pl.BlockSpec(memory_space=pltpu.SMEM)] + [anywhere] * 4 + [whole] * len(came),
        out_specs=[whole] * ways,
        out_shape=outs,
        scratch_shapes=[pltpu.SemaphoreType.DMA((len(slots), 2))],
        compiler_params=pltpu.CompilerParams(vmem_limit_bytes=SMALL_VMEM),
        cost_estimate=pl.CostEstimate(
            flops=0, bytes_accessed=2 * 2**20, transcendentals=0
        ),
        name=name,
    )(where, *map(in_hbm, maps[:2]), *maps[2:], *came)


def rank_kernel(where, hidden_ref, base_ref, *refs):
    maps, came, (mine_out, others_out, held, sem) = refs[:4], refs[4:8], refs[8:]
    depth = hidden_ref.shape[1]
    height = held.shape[1] - depth
    waits = []
    for r in range(2):
        adapter = owner(where, where[PLANE], r)
        _, start, wait = when_mine(where, adapter, maps, held.at[r], sem.at[r])
        start()
        waits.append(wait)
        away = lax.rem(where[PLANE] + 8 - adapter // 8, 8)
        odd = away % 2 == 1
        below = away <= 4 if r == 0 else away < 4
        above = jnp.logical_not(below)
        even = jnp.logical_and(away != 0, jnp.logical_not(odd))
        for source, chosen in zip(
            came,
            (
                jnp.logical_and(odd, below),
                jnp.logical_and(even, below),
                jnp.logical_and(odd, above),
                jnp.logical_and(even, above),
            ),
        ):

            @pl.when(chosen)
            def _(r=r, source=source):
                held[r] = source[r]

    half = where[HALF]
    for out, request in ((mine_out, half), (others_out, 1 - half)):
        rows = pl.ds(pl.multiple_of(request * NEW_TOK, NEW_TOK), NEW_TOK)
        for part in range(4):
            start = NEW_TOK + height + part * NEW_TOK
            out[start : start + NEW_TOK] = base_ref[rows, part * WIDTH : (part + 1) * WIDTH]
    for wait in waits:
        wait()
    for out, request in ((mine_out, half), (others_out, 1 - half)):
        rows = pl.ds(pl.multiple_of(request * NEW_TOK, NEW_TOK), NEW_TOK)
        out[:NEW_TOK] = jnp.dot(
            hidden_ref[rows], held[request, :depth], preferred_element_type=F32
        ).astype(BF)
        out[NEW_TOK : NEW_TOK + height] = held[request, depth:]


def rank_parts(where, hidden, base, maps, came):
    height = came[0].shape[1]
    out = jax.ShapeDtypeStruct((5 * NEW_TOK + height - hidden.shape[1], WIDTH), BF)
    anywhere = pl.BlockSpec(memory_space=pl.ANY)
    whole = pl.BlockSpec(memory_space=pltpu.VMEM)
    return pl.pallas_call(
        rank_kernel,
        in_specs=[pl.BlockSpec(memory_space=pltpu.SMEM), whole, whole]
        + [anywhere] * 4
        + [whole] * 4,
        out_specs=[whole, whole],
        out_shape=[out, out],
        scratch_shapes=[pltpu.VMEM((2, height, WIDTH), BF), pltpu.SemaphoreType.DMA((2, 2))],
        compiler_params=pltpu.CompilerParams(vmem_limit_bytes=SMALL_VMEM),
        name="rank_partial",
    )(where, hidden, base, *map(in_hbm, maps[:2]), *maps[2:], *came)


def seq_kernel(where, *refs):
    parts, (rank_out, base_out, up_out) = refs[:4], refs[4:]
    after = NEW_TOK + up_out.shape[1]
    rank_out[...] = sum(part[:NEW_TOK].astype(F32) for part in parts).astype(BF)
    for step, part in enumerate(parts):
        up_out[jnp.bitwise_xor(where[SEQ], step)] = part[NEW_TOK:after]
    for col in range(4):
        start = after + col * NEW_TOK
        base_out[:, col * WIDTH : (col + 1) * WIDTH] = sum(
            part[start : start + NEW_TOK].astype(F32) for part in parts
        )


def seq_sum(where, parts):
    whole = pl.BlockSpec(memory_space=pltpu.VMEM)
    return pl.pallas_call(
        seq_kernel,
        in_specs=[pl.BlockSpec(memory_space=pltpu.SMEM)] + [whole] * 4,
        out_specs=[whole] * 3,
        out_shape=[
            jax.ShapeDtypeStruct((NEW_TOK, WIDTH), BF),
            jax.ShapeDtypeStruct((NEW_TOK, 4 * WIDTH), F32),
            jax.ShapeDtypeStruct((4, parts[0].shape[0] - 5 * NEW_TOK, WIDTH), BF),
        ],
        compiler_params=pltpu.CompilerParams(vmem_limit_bytes=SMALL_VMEM),
        name="seq_sum",
    )(where, *parts)


def merge_kernel(*refs):
    parts, mean_out, log_out = refs[:4], refs[4], refs[5]
    half = parts[0].shape[0]
    tops = []
    for part in parts:
        packed = part[:, 16 * WIDTH :].astype(F32)
        tops.append(packed + pltpu.roll(packed, WIDTH - 16, 1) + pltpu.roll(packed, WIDTH - 32, 1))
    top = functools.reduce(jnp.maximum, tops)
    weights = [jnp.exp2(l - top) for l in tops]
    total = sum(weights)
    merged = top + jnp.log2(total)
    weights = [w / total for w in weights]
    for n in range(16):
        rows = slice(n * half, (n + 1) * half)
        cols = slice(n * WIDTH, (n + 1) * WIDTH)
        mean_out[rows] = sum(
            w[:, n : n + 1] * part[:, cols].astype(F32) for w, part in zip(weights, parts)
        )
        log_out[rows] = jnp.broadcast_to(merged[:, n : n + 1], (half, WIDTH))


def merge(parts):
    out = jax.ShapeDtypeStruct((16 * parts[0].shape[0], WIDTH), F32)
    whole = pl.BlockSpec(memory_space=pltpu.VMEM)
    return pl.pallas_call(
        merge_kernel,
        in_specs=[whole] * 4,
        out_specs=[whole, whole],
        out_shape=[out, out],
        compiler_params=pltpu.CompilerParams(vmem_limit_bytes=SMALL_VMEM),
        name="merge_prefix",
    )(*parts)


def final_kernel(where, q_ref, cos_ref, sin_ref, up_ref, mean_ref, log_ref, base_ref, *rest):
    ranks, (kv_out, attention_out, wide) = rest[:4], rest[4:]
    half = q_ref.shape[0]
    start = pl.multiple_of(where[PARITY] * half, half)
    rank = sum(r[...].astype(F32) for r in ranks).astype(BF)
    keys, values = [], []
    for h in range(2):
        for e in range(2):
            delta = jnp.dot(
                rank[:, e * 64 : (e + 1) * 64], up_ref[2 * e + h], preferred_element_type=F32
            )
            part = 2 * h + e
            field = base_ref[:, part * WIDTH : (part + 1) * WIDTH] + delta
            if e == 0:
                field = field * cos_ref[...] + pltpu.roll(field, WIDTH // 2, 1) * sin_ref[...]
            wide[pl.ds(part, NEW_TOK, stride=4), :] = field
            (keys, values)[e].append(field.astype(BF))
    kv_out[...] = wide[pl.ds(start * 4, half * 4), :].astype(BF)
    rows = 8 * half
    token = lax.broadcasted_iota(jnp.int32, (rows, NEW_TOK), 0) % half + start
    seen = lax.broadcasted_iota(jnp.int32, (rows, NEW_TOK), 1) <= token
    ones = jnp.ones((NEW_TOK, WIDTH), BF)
    for h in range(2):
        q = jnp.concatenate(
            [q_ref[:, n * WIDTH : (n + 1) * WIDTH] for n in range(h * 8, h * 8 + 8)], axis=0
        )
        s = lax.dot_general(q, keys[h], (((1,), (1,)), ((), ())), preferred_element_type=F32)
        s = jnp.where(seen, s * SCALE, LOW)
        block = slice(h * rows, (h + 1) * rows)
        log = log_ref[block]
        top = jnp.maximum(log, jnp.max(s, axis=1, keepdims=True))
        weight = jnp.exp2(log - top)
        p = jnp.exp2(s - top).astype(BF)
        value = jnp.dot(
            p, jnp.concatenate([values[h], ones], axis=1), preferred_element_type=F32
        )
        out = (value[:, :WIDTH] + weight * mean_ref[block]) / (value[:, WIDTH:] + weight)
        out = out.astype(BF)
        for j in range(8):
            n = h * 8 + j
            attention_out[:, n * WIDTH : (n + 1) * WIDTH] = out[j * half : (j + 1) * half]


def final(where, queries, cos, sin, up, mean, log, base, ranks):
    half, width = NEW_TOK // 2, queries.shape[1]

    def whole(a):
        return pl.BlockSpec(a.shape, lambda i, w: (0,) * a.ndim)

    rest = [cos, sin, up, mean, log, base, *ranks]
    return pl.pallas_call(
        final_kernel,
        grid_spec=pltpu.PrefetchScalarGridSpec(
            num_scalar_prefetch=1,
            grid=(1,),
            in_specs=[pl.BlockSpec((half, width), lambda i, w: (w[SEQ], 0))]
            + [whole(a) for a in rest],
            out_specs=[
                pl.BlockSpec((half * 4, WIDTH), lambda i, w: (0, 0)),
                pl.BlockSpec((half, width), lambda i, w: (0, 0)),
            ],
            scratch_shapes=[pltpu.VMEM((NEW_TOK * 4, WIDTH), F32)],
        ),
        out_shape=[
            jax.ShapeDtypeStruct((half * 4, WIDTH), BF),
            jax.ShapeDtypeStruct((half, width), BF),
        ],
        compiler_params=pltpu.CompilerParams(vmem_limit_bytes=SMALL_VMEM),
        name="new_kv_and_attention",
    )(where, queries, *rest)


def rotary_tables():
    exponents = jnp.arange(WIDTH // 2, dtype=F32)
    frequency = jnp.exp(exponents * (-2.0 * math.log(500000.0) / WIDTH))
    positions = CACHE + jnp.arange(NEW_TOK, dtype=jnp.int32)
    angles = positions.astype(F32)[:, None] * frequency[None, :]
    cos, sin = jnp.cos(angles), jnp.sin(angles)
    return jnp.concatenate([cos, cos], axis=1), jnp.concatenate([-sin, sin], axis=1)


def flip(axis, mask):
    return lambda a: lax.ppermute(
        a, axis, [(i, i ^ mask) for i in range(lax.axis_size(axis))]
    )


def shift(axis, step):
    size = lax.axis_size(axis)
    return lambda a: lax.ppermute(a, axis, [(i, (i + step) % size) for i in range(size)])


def tie(value, *others):
    return lax.optimization_barrier((value, *others))[0]


def local(
    hidden,
    key_value_weight,
    adapter_down_weight,
    adapter_up_weight,
    queries,
    key_value_cache,
    request_adapter,
):
    seq, group, tensor = (lax.axis_index(a) for a in ("seq", "group", "tensor"))
    place = jnp.stack([seq, seq // 2, seq % 2, tensor, group // 2, group % 2])
    where = jnp.concatenate([place.astype(jnp.int32), request_adapter])

    maps = [adapter_down_weight, adapter_up_weight]
    maps += [flip("group", 1)(a) for a in maps]

    far = [(0, 0, 3, 0, None), (0, 1, 3, 1, None), (0, 2, 4, 0, None)]
    far += [(1, 0, -3, 0, None), (1, 1, -3, 1, None), (1, 2, -4, 1, None)]
    near = [(0, 0, 1, 0, (0, 0)), (0, 1, 1, 1, (0, 1)), (1, 0, 2, 0, (0, 2)), (1, 1, 2, 1, None)]
    near += [(2, 0, -1, 0, (1, 0)), (2, 1, -1, 1, (1, 1))]
    near += [(3, 0, -2, 0, None), (3, 1, -2, 1, (1, 2))]

    sent = relay(where, maps, [], far, "relay_far")
    came = [shift("group", 4)(sent[0]), shift("group", -4)(sent[1])]

    cache_rows = key_value_cache.reshape(-1, WIDTH)
    *parts, cache_rows, queries = prep(
        tie(where, *sent), hidden, key_value_weight.reshape(-1, WIDTH), cache_rows, queries
    )
    received = [shift("tensor", step)(parts[step]) for step in (1, 2, 3)]
    o2, o3 = attend(tie(where, parts[0]), queries, cache_rows, True)

    sent = relay(tie(where, o2), maps, came, near, "relay_near")
    came = [shift("group", 2 * hops)(a) for hops, a in zip((1, 2, -1, -2), sent)]
    received = lax.optimization_barrier((*received, *sent))[:3]
    base = (parts[0].astype(F32) + sum(r.astype(F32) for r in received)).astype(BF)
    got2 = flip("seq", 2)(tie(o2, *sent))
    o0, o1 = attend(tie(where, *sent, base), queries, cache_rows, False)

    cos, sin = rotary_tables()
    mine, others = rank_parts(tie(where, o1, cos, sin, got2), hidden, base, maps, came)
    rank, base, ups = seq_sum(
        where, [mine, flip("seq", 1)(mine), flip("seq", 2)(others), flip("seq", 3)(others)]
    )
    got1, got3 = flip("seq", 1)(tie(o1, rank)), flip("seq", 3)(tie(o3, rank))
    ranks = [rank] + [shift("tensor", step)(rank) for step in (1, 2, 3)]
    mean, log = merge(list(lax.optimization_barrier((o0, got1, got2, got3, rank)))[:4])

    new_kv, attention = final(where, queries, cos, sin, ups, mean, log, base, ranks)
    return new_kv.reshape(-1, 2, 2, WIDTH), attention


def solution(mesh):
    in_specs = (
        P("group", ("tensor", "seq")),
        P(("tensor", "seq"), None, None, None),
        P("group", ("tensor", "seq"), None),
        P("group", None, None, "tensor"),
        P("group", "tensor"),
        P("group", "seq", "tensor", None, None),
        P(),
    )
    out_specs = (P(("group", "seq"), "tensor", None, None), P(("group", "seq"), "tensor"))
    return jax.shard_map(local, mesh=mesh, in_specs=in_specs, out_specs=out_specs, check_vma=False)
```

```python
import functools
import math

import jax
import jax.numpy as jnp
from jax import lax
from jax.experimental import pallas as pl
from jax.experimental.pallas import tpu as pltpu
from jax.sharding import PartitionSpec as P

NEW_TOK = 128
CACHE = 16384
WIDTH = 128
SCALE = math.log2(math.e) / math.sqrt(WIDTH)
KEY_BLOCK = 4096
BODY = 4
TILE = 256
LOW = -1e30
BF = jnp.bfloat16
F32 = jnp.float32
ATTEND_VMEM = 44 * 2**20
SMALL_VMEM = 16 * 2**20

SEQ, HALF, PARITY, TENSOR, PLANE, CORE, ADAPTERS = 0, 1, 2, 3, 4, 5, 6


def prep_kernel(where, hidden_far, weight_far, cache_far, query_far, *rest):
    outs, (cache_out, query_out, hidden_ref, weight_ref, cols, sem) = rest[:4], rest[4:]
    loads = [
        pltpu.make_async_copy(far, near, sem.at[n])
        for n, (far, near) in enumerate(
            (
                (weight_far, weight_ref),
                (hidden_far, hidden_ref),
                (query_far, query_out),
                (cache_far, cache_out),
            )
        )
    ]
    for load in loads:
        load.start()
    for load in loads[:2]:
        load.wait()
    depth = hidden_ref.shape[1]
    rows = weight_ref[...].astype(F32).reshape(depth // 8, 8, 2, 8, WIDTH)
    place = lax.broadcasted_iota(jnp.int32, (depth // 8, 8, WIDTH), 1)
    for a in range(2):
        parts = [rows[:, j, a] for j in range(8)]
        for bit in (1, 2, 4):
            odd = (place & bit) != 0
            for j in range(8):
                if not j & bit:
                    low, high = parts[j], parts[j | bit]
                    parts[j] = jnp.where(odd, pltpu.roll(high, bit, 1), low)
                    parts[j | bit] = jnp.where(odd, high, pltpu.roll(low, 8 - bit, 1))
        for c in range(8):
            dest, part = 2 * a + c // 4, c % 4
            cols[dest, :, part * WIDTH : (part + 1) * WIDTH] = (
                parts[c].reshape(depth, WIDTH).astype(BF)
            )
    for step in range(4):
        dest = lax.rem(where[TENSOR] + step, 4)
        outs[step][...] = jnp.dot(
            hidden_ref[...], cols[dest], preferred_element_type=F32
        ).astype(BF)
    for load in loads[2:]:
        load.wait()


def in_hbm(a):
    return pltpu.with_memory_space_constraint(a, pltpu.HBM)


def prep(where, hidden, weight_rows, cache_rows, queries):
    tokens, depth = hidden.shape
    whole = pl.BlockSpec(memory_space=pltpu.VMEM)
    anywhere = pl.BlockSpec(memory_space=pl.ANY)
    return pl.pallas_call(
        prep_kernel,
        in_specs=[pl.BlockSpec(memory_space=pltpu.SMEM)] + [anywhere] * 4,
        out_specs=[whole] * 6,
        out_shape=[jax.ShapeDtypeStruct((tokens, 4 * WIDTH), BF)] * 4
        + [pltpu.VMEM(cache_rows.shape, BF), pltpu.VMEM(queries.shape, BF)],
        scratch_shapes=[
            pltpu.VMEM(hidden.shape, BF),
            pltpu.VMEM(weight_rows.shape, BF),
            pltpu.VMEM((4, depth, 4 * WIDTH), BF),
            pltpu.SemaphoreType.DMA((4,)),
        ],
        compiler_params=pltpu.CompilerParams(vmem_limit_bytes=SMALL_VMEM),
        cost_estimate=pl.CostEstimate(
            flops=2 * tokens * depth * 16 * WIDTH, bytes_accessed=11 * 2**20, transcendentals=0
        ),
        name="base_partial",
    )(where, *map(in_hbm, (hidden, weight_rows, cache_rows, queries)))


def attend_kernel(where, q_ref, x_ref, o_first, o_second, acc, top, wide, keys, values):
    block = pl.program_id(0)
    tokens = q_ref.shape[0]
    per_tile = TILE // tokens
    tiles = 8 // per_tile

    @pl.when(block == 0)
    def _():
        acc[...] = jnp.zeros_like(acc)
        top[...] = jnp.full_like(top, LOW)
        for h in range(2):
            values[h, :, WIDTH:] = jnp.ones((KEY_BLOCK, WIDTH), BF)

    wide[...] = x_ref[...].astype(F32)
    for h in range(2):
        keys[h] = wide[pl.ds(2 * h, KEY_BLOCK, stride=4), :].astype(BF)
        values[h, :, :WIDTH] = wide[pl.ds(2 * h + 1, KEY_BLOCK, stride=4), :].astype(BF)

    def score(h, t):
        first = h * 8 + t * per_tile
        q = jnp.concatenate(
            [
                q_ref[:, pl.ds(pl.multiple_of((first + j) * WIDTH, WIDTH), WIDTH)]
                for j in range(per_tile)
            ],
            axis=0,
        )
        return lax.dot_general(q, keys[h], (((1,), (1,)), ((), ())), preferred_element_type=F32)

    def absorb(h, t, s):
        i = h * tiles + t
        before = top[i]
        after = jnp.maximum(before, jnp.max(s, axis=1, keepdims=True) * SCALE)
        top[i] = after
        fade = jnp.exp2(before - after)
        p = jnp.exp2(s * SCALE - after[:, :1]).astype(BF)
        acc[i] = acc[i] * jnp.concatenate([fade, fade], axis=1) + jnp.dot(
            p, values[h], preferred_element_type=F32
        )

    def turn(k, _):
        h, start = k // (tiles // BODY), k % (tiles // BODY) * BODY
        ahead = []
        for t in range(0, BODY, 2):
            now = [(start + u, score(h, start + u)) for u in (t, t + 1)]
            for job in ahead:
                absorb(h, *job)
            ahead = now
        for job in ahead:
            absorb(h, *job)
        return 0

    lax.fori_loop(0, 2 * tiles // BODY, turn, 0)

    @pl.when(block == pl.num_programs(0) - 1)
    def _():
        half = tokens // 2
        odd = where[PARITY] == 1
        lane = lax.broadcasted_iota(jnp.int32, (tokens, WIDTH), 1)
        logs = jnp.zeros((tokens, WIDTH), F32)
        for h in range(2):
            for t in range(tiles):
                i = h * tiles + t
                total = acc[i, :, WIDTH:]
                mean = (acc[i, :, :WIDTH] / total).astype(BF)
                log = top[i] + jnp.log2(total)
                for j in range(per_tile):
                    n = h * 8 + t * per_tile + j
                    early = mean[j * tokens : j * tokens + half]
                    late = mean[j * tokens + half : (j + 1) * tokens]
                    cols = slice(n * WIDTH, (n + 1) * WIDTH)
                    o_first[:, cols] = jnp.where(odd, late, early)
                    o_second[:, cols] = jnp.where(odd, early, late)
                    logs = jnp.where(lane == n, log[j * tokens : (j + 1) * tokens], logs)
        high = logs.astype(BF).astype(F32)
        middle = (logs - high).astype(BF).astype(F32)
        low = logs - high - middle
        logs = (high + pltpu.roll(middle, 16, 1) + pltpu.roll(low, 32, 1)).astype(BF)
        o_first[:, 16 * WIDTH :] = jnp.where(odd, logs[half:], logs[:half])
        o_second[:, 16 * WIDTH :] = jnp.where(odd, logs[:half], logs[half:])


def attend(where, queries, cache_rows, other):
    tokens, width = NEW_TOK, queries.shape[1]
    blocks = cache_rows.shape[0] // 2 // 4 // KEY_BLOCK
    tiles = 16 * tokens // TILE

    def request(w):
        return 1 - w[HALF] if other else w[HALF]

    o = jax.ShapeDtypeStruct((tokens // 2, width + WIDTH), BF)
    scores = 16 * tokens * blocks * KEY_BLOCK
    return pl.pallas_call(
        attend_kernel,
        grid_spec=pltpu.PrefetchScalarGridSpec(
            num_scalar_prefetch=1,
            grid=(blocks,),
            in_specs=[
                pl.BlockSpec((tokens, width), lambda i, w: (request(w), 0)),
                pl.BlockSpec((KEY_BLOCK * 4, WIDTH), lambda i, w: (request(w) * blocks + i, 0)),
            ],
            out_specs=[pl.BlockSpec(o.shape, lambda i, w: (0, 0))] * 2,
            scratch_shapes=[
                pltpu.VMEM((tiles, TILE, 2 * WIDTH), F32),
                pltpu.VMEM((tiles, TILE, WIDTH), F32),
                pltpu.VMEM((KEY_BLOCK * 4, WIDTH), F32),
                pltpu.VMEM((2, KEY_BLOCK, WIDTH), BF),
                pltpu.VMEM((2, KEY_BLOCK, 2 * WIDTH), BF),
            ],
        ),
        out_shape=[o, o],
        compiler_params=pltpu.CompilerParams(vmem_limit_bytes=ATTEND_VMEM),
        cost_estimate=pl.CostEstimate(
            flops=scores * WIDTH * 8, bytes_accessed=5 * 2**20, transcendentals=scores
        ),
        name="attend_other" if other else "attend_own",
    )(where, queries, cache_rows)


def owner(where, plane, r):
    return where[ADAPTERS + 2 * (2 * plane + where[CORE]) + r]


def when_mine(where, adapter, maps, out, sem):
    down, up, mate_down, mate_up = maps
    mine = adapter // 8 == where[PLANE]
    mates = adapter // 4 % 2 != where[CORE]
    k = adapter % 4
    depth = down.shape[1]
    cols = pl.ds(pl.multiple_of(where[PARITY] * WIDTH, WIDTH), WIDTH)

    def pair(downs, ups):
        return (
            pltpu.make_async_copy(downs.at[k], out.at[:depth], sem.at[0]),
            pltpu.make_async_copy(ups.at[k, where[HALF], :, cols], out.at[depth:], sem.at[1]),
        )

    def start():
        @pl.when(jnp.logical_and(mine, mates))
        def _():
            for copy in pair(mate_down, mate_up):
                copy.start()

        @pl.when(jnp.logical_and(mine, jnp.logical_not(mates)))
        def _():
            for copy in pair(down, up):
                copy.start()

    def wait():
        @pl.when(mine)
        def _():
            for copy in pair(down, up):
                copy.wait()

    return mine, start, wait


def relay_kernel(slots, arrivals, where, *refs):
    maps, came, outs, sem = refs[:4], refs[4 : 4 + arrivals], refs[4 + arrivals : -1], refs[-1]
    waits = []
    for n, (way, slot, hops, r, arrival) in enumerate(slots):
        plane = lax.rem(where[PLANE] + hops + 8, 8)
        out = outs[way].at[slot]
        mine, start, wait = when_mine(where, owner(where, plane, r), maps, out, sem.at[n])
        start()
        waits.append(wait)
        if arrival is not None:

            @pl.when(jnp.logical_not(mine))
            def _(out=out, arrival=arrival):
                out[...] = came[arrival[0]][arrival[1]]

    for wait in waits:
        wait()


def relay(where, maps, came, slots, name):
    height = maps[0].shape[1] + maps[1].shape[2]
    ways = 1 + max(slot[0] for slot in slots)
    outs = [
        jax.ShapeDtypeStruct((sum(slot[0] == way for slot in slots), height, WIDTH), BF)
        for way in range(ways)
    ]
    anywhere = pl.BlockSpec(memory_space=pl.ANY)
    whole = pl.BlockSpec(memory_space=pltpu.VMEM)
    return pl.pallas_call(
        functools.partial(relay_kernel, slots, len(came)),
        in_specs=[pl.BlockSpec(memory_space=pltpu.SMEM)] + [anywhere] * 4 + [whole] * len(came),
        out_specs=[whole] * ways,
        out_shape=outs,
        scratch_shapes=[pltpu.SemaphoreType.DMA((len(slots), 2))],
        compiler_params=pltpu.CompilerParams(vmem_limit_bytes=SMALL_VMEM),
        cost_estimate=pl.CostEstimate(
            flops=0, bytes_accessed=2 * 2**20, transcendentals=0
        ),
        name=name,
    )(where, *map(in_hbm, maps[:2]), *maps[2:], *came)


def rank_kernel(where, hidden_ref, *refs):
    maps, came, (rank_out, up_out, held, sem) = refs[:4], refs[4:8], refs[8:]
    depth = hidden_ref.shape[1]
    waits = []
    for r in range(2):
        adapter = owner(where, where[PLANE], r)
        _, start, wait = when_mine(where, adapter, maps, held.at[r], sem.at[r])
        start()
        waits.append(wait)
        away = lax.rem(where[PLANE] + 8 - adapter // 8, 8)
        odd = away % 2 == 1
        below = away <= 4 if r == 0 else away < 4
        above = jnp.logical_not(below)
        even = jnp.logical_and(away != 0, jnp.logical_not(odd))
        for source, chosen in zip(
            came,
            (
                jnp.logical_and(odd, below),
                jnp.logical_and(even, below),
                jnp.logical_and(odd, above),
                jnp.logical_and(even, above),
            ),
        ):

            @pl.when(chosen)
            def _(r=r, source=source):
                held[r] = source[r]

    for r in range(2):
        waits[r]()
        rank_out[r * NEW_TOK : (r + 1) * NEW_TOK] = jnp.dot(
            hidden_ref[r * NEW_TOK : (r + 1) * NEW_TOK],
            held[r, :depth],
            preferred_element_type=F32,
        ).astype(BF)
        up_out[r] = held[r, depth:]


def rank_parts(where, hidden, maps, came):
    height = came[0].shape[1]
    anywhere = pl.BlockSpec(memory_space=pl.ANY)
    whole = pl.BlockSpec(memory_space=pltpu.VMEM)
    return pl.pallas_call(
        rank_kernel,
        in_specs=[pl.BlockSpec(memory_space=pltpu.SMEM), whole]
        + [anywhere] * 4
        + [whole] * 4,
        out_specs=[whole, whole],
        out_shape=[
            jax.ShapeDtypeStruct((hidden.shape[0], WIDTH), BF),
            jax.ShapeDtypeStruct((2, height - hidden.shape[1], WIDTH), BF),
        ],
        scratch_shapes=[pltpu.VMEM((2, height, WIDTH), BF), pltpu.SemaphoreType.DMA((2, 2))],
        compiler_params=pltpu.CompilerParams(vmem_limit_bytes=SMALL_VMEM),
        name="rank_partial",
    )(where, hidden, *map(in_hbm, maps[:2]), *maps[2:], *came)


def parcel_kernel(where, base_ref, got_ref, up_ref, *refs):
    ranks, outs = refs[:4], refs[4:]
    after = NEW_TOK + up_ref.shape[1]
    half = where[HALF]
    for out, request in zip(outs, (half, 1 - half)):
        rows = pl.ds(pl.multiple_of(request * NEW_TOK, NEW_TOK), NEW_TOK)
        out[:NEW_TOK] = sum(rank[rows].astype(F32) for rank in ranks).astype(BF)
        out[NEW_TOK:after] = up_ref[request]
    rows = pl.ds(pl.multiple_of(half * NEW_TOK, NEW_TOK), NEW_TOK)
    for part in range(4):
        start = after + part * NEW_TOK
        cols = slice(part * WIDTH, (part + 1) * WIDTH)
        outs[0][start : start + NEW_TOK] = (
            base_ref[rows, cols].astype(F32) + got_ref[:, cols].astype(F32)
        ).astype(BF)


def parcels(where, base, got, ups, ranks):
    whole = pl.BlockSpec(memory_space=pltpu.VMEM)
    height = NEW_TOK + ups.shape[1]
    return pl.pallas_call(
        parcel_kernel,
        in_specs=[pl.BlockSpec(memory_space=pltpu.SMEM)] + [whole] * 7,
        out_specs=[whole, whole],
        out_shape=[
            jax.ShapeDtypeStruct((height + 4 * NEW_TOK, WIDTH), BF),
            jax.ShapeDtypeStruct((height, WIDTH), BF),
        ],
        compiler_params=pltpu.CompilerParams(vmem_limit_bytes=SMALL_VMEM),
        name="tensor_sum",
    )(where, base, got, ups, *ranks)


def merge_kernel(*refs):
    parts, mean_out, log_out = refs[:4], refs[4], refs[5]
    half = parts[0].shape[0]
    tops = []
    for part in parts:
        packed = part[:, 16 * WIDTH :].astype(F32)
        tops.append(packed + pltpu.roll(packed, WIDTH - 16, 1) + pltpu.roll(packed, WIDTH - 32, 1))
    top = functools.reduce(jnp.maximum, tops)
    weights = [jnp.exp2(l - top) for l in tops]
    total = sum(weights)
    merged = top + jnp.log2(total)
    weights = [w / total for w in weights]
    for n in range(16):
        rows = slice(n * half, (n + 1) * half)
        cols = slice(n * WIDTH, (n + 1) * WIDTH)
        mean_out[rows] = sum(
            w[:, n : n + 1] * part[:, cols].astype(F32) for w, part in zip(weights, parts)
        )
        log_out[rows] = jnp.broadcast_to(merged[:, n : n + 1], (half, WIDTH))


def merge(parts):
    out = jax.ShapeDtypeStruct((16 * parts[0].shape[0], WIDTH), F32)
    whole = pl.BlockSpec(memory_space=pltpu.VMEM)
    return pl.pallas_call(
        merge_kernel,
        in_specs=[whole] * 4,
        out_specs=[whole, whole],
        out_shape=[out, out],
        compiler_params=pltpu.CompilerParams(vmem_limit_bytes=SMALL_VMEM),
        name="merge_prefix",
    )(*parts)


def final_kernel(where, q_ref, cos_ref, sin_ref, mean_ref, log_ref, *rest):
    parts, (kv_out, attention_out, wide, up_ref) = rest[:4], rest[4:]
    half = q_ref.shape[0]
    start = pl.multiple_of(where[PARITY] * half, half)
    after = NEW_TOK + up_ref.shape[1]
    rank = sum(part[:NEW_TOK].astype(F32) for part in parts).astype(BF)
    for step, part in enumerate(parts):
        up_ref[jnp.bitwise_xor(where[SEQ], step)] = part[NEW_TOK:after]
    base = [
        sum(
            part[after + col * NEW_TOK : after + (col + 1) * NEW_TOK].astype(F32)
            for part in parts[:2]
        )
        for col in range(4)
    ]
    keys, values = [], []
    for h in range(2):
        for e in range(2):
            delta = jnp.dot(
                rank[:, e * 64 : (e + 1) * 64], up_ref[2 * e + h], preferred_element_type=F32
            )
            part = 2 * h + e
            field = base[part] + delta
            if e == 0:
                field = field * cos_ref[...] + pltpu.roll(field, WIDTH // 2, 1) * sin_ref[...]
            wide[pl.ds(part, NEW_TOK, stride=4), :] = field
            (keys, values)[e].append(field.astype(BF))
    kv_out[...] = wide[pl.ds(start * 4, half * 4), :].astype(BF)
    rows = 8 * half
    token = lax.broadcasted_iota(jnp.int32, (rows, NEW_TOK), 0) % half + start
    seen = lax.broadcasted_iota(jnp.int32, (rows, NEW_TOK), 1) <= token
    ones = jnp.ones((NEW_TOK, WIDTH), BF)
    for h in range(2):
        q = jnp.concatenate(
            [q_ref[:, n * WIDTH : (n + 1) * WIDTH] for n in range(h * 8, h * 8 + 8)], axis=0
        )
        s = lax.dot_general(q, keys[h], (((1,), (1,)), ((), ())), preferred_element_type=F32)
        s = jnp.where(seen, s * SCALE, LOW)
        block = slice(h * rows, (h + 1) * rows)
        log = log_ref[block]
        top = jnp.maximum(log, jnp.max(s, axis=1, keepdims=True))
        weight = jnp.exp2(log - top)
        p = jnp.exp2(s - top).astype(BF)
        value = jnp.dot(
            p, jnp.concatenate([values[h], ones], axis=1), preferred_element_type=F32
        )
        out = (value[:, :WIDTH] + weight * mean_ref[block]) / (value[:, WIDTH:] + weight)
        out = out.astype(BF)
        for j in range(8):
            n = h * 8 + j
            attention_out[:, n * WIDTH : (n + 1) * WIDTH] = out[j * half : (j + 1) * half]


def final(where, queries, cos, sin, mean, log, parts):
    half, width = NEW_TOK // 2, queries.shape[1]

    def whole(a):
        return pl.BlockSpec(a.shape, lambda i, w: (0,) * a.ndim)

    rest = [cos, sin, mean, log, *parts]
    return pl.pallas_call(
        final_kernel,
        grid_spec=pltpu.PrefetchScalarGridSpec(
            num_scalar_prefetch=1,
            grid=(1,),
            in_specs=[pl.BlockSpec((half, width), lambda i, w: (w[SEQ], 0))]
            + [whole(a) for a in rest],
            out_specs=[
                pl.BlockSpec((half * 4, WIDTH), lambda i, w: (0, 0)),
                pl.BlockSpec((half, width), lambda i, w: (0, 0)),
            ],
            scratch_shapes=[
                pltpu.VMEM((NEW_TOK * 4, WIDTH), F32),
                pltpu.VMEM((4, parts[0].shape[0] - 5 * NEW_TOK, WIDTH), BF),
            ],
        ),
        out_shape=[
            jax.ShapeDtypeStruct((half * 4, WIDTH), BF),
            jax.ShapeDtypeStruct((half, width), BF),
        ],
        compiler_params=pltpu.CompilerParams(vmem_limit_bytes=SMALL_VMEM),
        name="new_kv_and_attention",
    )(where, queries, *rest)


def rotary_tables():
    exponents = jnp.arange(WIDTH // 2, dtype=F32)
    frequency = jnp.exp(exponents * (-2.0 * math.log(500000.0) / WIDTH))
    positions = CACHE + jnp.arange(NEW_TOK, dtype=jnp.int32)
    angles = positions.astype(F32)[:, None] * frequency[None, :]
    cos, sin = jnp.cos(angles), jnp.sin(angles)
    return jnp.concatenate([cos, cos], axis=1), jnp.concatenate([-sin, sin], axis=1)


def flip(axis, mask):
    return lambda a: lax.ppermute(
        a, axis, [(i, i ^ mask) for i in range(lax.axis_size(axis))]
    )


def shift(axis, step):
    size = lax.axis_size(axis)
    return lambda a: lax.ppermute(a, axis, [(i, (i + step) % size) for i in range(size)])


def tie(value, *others):
    return lax.optimization_barrier((value, *others))[0]


def local(
    hidden,
    key_value_weight,
    adapter_down_weight,
    adapter_up_weight,
    queries,
    key_value_cache,
    request_adapter,
):
    seq, group, tensor = (lax.axis_index(a) for a in ("seq", "group", "tensor"))
    place = jnp.stack([seq, seq // 2, seq % 2, tensor, group // 2, group % 2])
    where = jnp.concatenate([place.astype(jnp.int32), request_adapter])

    maps = [adapter_down_weight, adapter_up_weight]
    maps += [flip("group", 1)(a) for a in maps]

    far = [(0, 0, 3, 0, None), (0, 1, 3, 1, None), (0, 2, 4, 0, None)]
    far += [(1, 0, -3, 0, None), (1, 1, -3, 1, None), (1, 2, -4, 1, None)]
    near = [(0, 0, 1, 0, (0, 0)), (0, 1, 1, 1, (0, 1)), (1, 0, 2, 0, (0, 2)), (1, 1, 2, 1, None)]
    near += [(2, 0, -1, 0, (1, 0)), (2, 1, -1, 1, (1, 1))]
    near += [(3, 0, -2, 0, None), (3, 1, -2, 1, (1, 2))]

    sent = relay(where, maps, [], far, "relay_far")
    came = [shift("group", 4)(sent[0]), shift("group", -4)(sent[1])]

    cache_rows = key_value_cache.reshape(-1, WIDTH)
    *parts, cache_rows, queries = prep(
        tie(where, *sent), hidden, key_value_weight.reshape(-1, WIDTH), cache_rows, queries
    )
    received = [shift("tensor", step)(parts[step]) for step in (1, 2, 3)]
    o2, o3 = attend(tie(where, parts[0]), queries, cache_rows, True)

    sent = relay(tie(where, o2), maps, came, near, "relay_near")
    came = [shift("group", 2 * hops)(a) for hops, a in zip((1, 2, -1, -2), sent)]
    received = lax.optimization_barrier((*received, *sent))[:3]
    base = (parts[0].astype(F32) + sum(r.astype(F32) for r in received)).astype(BF)
    got2 = flip("seq", 2)(tie(o2, *sent))
    base_other = lax.dynamic_slice_in_dim(base, (1 - seq // 2) * NEW_TOK, NEW_TOK, 0)
    o0, o1 = attend(tie(where, *sent, base, base_other), queries, cache_rows, False)
    got_base = flip("seq", 3)(tie(base_other, o1))

    cos, sin = rotary_tables()
    rank, ups = rank_parts(tie(where, o1, cos, sin, got2), hidden, maps, came)
    got1, got3 = flip("seq", 1)(tie(o1, rank)), flip("seq", 3)(tie(o3, rank))
    ranks = [rank] + [shift("tensor", step)(rank) for step in (1, 2, 3)]
    mine, others = parcels(where, base, got_base, ups, ranks)
    parts = [mine, flip("seq", 1)(mine), flip("seq", 2)(others), flip("seq", 3)(others)]
    mean, log = merge(list(lax.optimization_barrier((o0, got1, got2, got3, mine)))[:4])

    new_kv, attention = final(where, queries, cos, sin, mean, log, parts)
    return new_kv.reshape(-1, 2, 2, WIDTH), attention


def solution(mesh):
    in_specs = (
        P("group", ("tensor", "seq")),
        P(("tensor", "seq"), None, None, None),
        P("group", ("tensor", "seq"), None),
        P("group", None, None, "tensor"),
        P("group", "tensor"),
        P("group", "seq", "tensor", None, None),
        P(),
    )
    out_specs = (P(("group", "seq"), "tensor", None, None), P(("group", "seq"), "tensor"))
    return jax.shard_map(local, mesh=mesh, in_specs=in_specs, out_specs=out_specs, check_vma=False)
```

```python
import functools
import math

import jax
import jax.numpy as jnp
from jax import lax
from jax.experimental import pallas as pl
from jax.experimental.pallas import tpu as pltpu
from jax.sharding import PartitionSpec as P

NEW_TOK = 128
CACHE = 16384
WIDTH = 128
SCALE = math.log2(math.e) / math.sqrt(WIDTH)
KEY_BLOCK = 4096
BODY = 4
TILE = 256
LOW = -1e30
BF = jnp.bfloat16
F32 = jnp.float32
ATTEND_VMEM = 44 * 2**20
SMALL_VMEM = 16 * 2**20

SEQ, HALF, PARITY, TENSOR, PLANE, CORE, ADAPTERS = 0, 1, 2, 3, 4, 5, 6


def prep_kernel(where, hidden_far, weight_far, cache_far, query_far, *rest):
    outs, (cache_out, query_out, hidden_ref, weight_ref, cols, sem) = rest[:4], rest[4:]
    loads = [
        pltpu.make_async_copy(far, near, sem.at[n])
        for n, (far, near) in enumerate(
            (
                (weight_far, weight_ref),
                (hidden_far, hidden_ref),
                (query_far, query_out),
                (cache_far, cache_out),
            )
        )
    ]
    for load in loads:
        load.start()
    for load in loads[:2]:
        load.wait()
    depth = hidden_ref.shape[1]
    rows = weight_ref[...].astype(F32).reshape(depth // 8, 8, 2, 8, WIDTH)
    place = lax.broadcasted_iota(jnp.int32, (depth // 8, 8, WIDTH), 1)
    for a in range(2):
        parts = [rows[:, j, a] for j in range(8)]
        for bit in (1, 2, 4):
            odd = (place & bit) != 0
            for j in range(8):
                if not j & bit:
                    low, high = parts[j], parts[j | bit]
                    parts[j] = jnp.where(odd, pltpu.roll(high, bit, 1), low)
                    parts[j | bit] = jnp.where(odd, high, pltpu.roll(low, 8 - bit, 1))
        for c in range(8):
            dest, part = 2 * a + c // 4, c % 4
            cols[dest, :, part * WIDTH : (part + 1) * WIDTH] = (
                parts[c].reshape(depth, WIDTH).astype(BF)
            )
    for step in range(4):
        dest = lax.rem(where[TENSOR] + step, 4)
        outs[step][...] = jnp.dot(
            hidden_ref[...], cols[dest], preferred_element_type=F32
        ).astype(BF)
    for load in loads[2:]:
        load.wait()


def in_hbm(a):
    return pltpu.with_memory_space_constraint(a, pltpu.HBM)


def prep(where, hidden, weight_rows, cache_rows, queries):
    tokens, depth = hidden.shape
    whole = pl.BlockSpec(memory_space=pltpu.VMEM)
    anywhere = pl.BlockSpec(memory_space=pl.ANY)
    return pl.pallas_call(
        prep_kernel,
        in_specs=[pl.BlockSpec(memory_space=pltpu.SMEM)] + [anywhere] * 4,
        out_specs=[whole] * 6,
        out_shape=[jax.ShapeDtypeStruct((tokens, 4 * WIDTH), BF)] * 4
        + [pltpu.VMEM(cache_rows.shape, BF), pltpu.VMEM(queries.shape, BF)],
        scratch_shapes=[
            pltpu.VMEM(hidden.shape, BF),
            pltpu.VMEM(weight_rows.shape, BF),
            pltpu.VMEM((4, depth, 4 * WIDTH), BF),
            pltpu.SemaphoreType.DMA((4,)),
        ],
        compiler_params=pltpu.CompilerParams(vmem_limit_bytes=SMALL_VMEM),
        cost_estimate=pl.CostEstimate(
            flops=2 * tokens * depth * 16 * WIDTH, bytes_accessed=11 * 2**20, transcendentals=0
        ),
        name="base_partial",
    )(where, *map(in_hbm, (hidden, weight_rows, cache_rows, queries)))


def attend_kernel(unroll, where, q_ref, x_ref, o_first, o_second, acc, top, wide, keys, values):
    block = pl.program_id(0)
    tokens = q_ref.shape[0]
    per_tile = TILE // tokens
    tiles = 8 // per_tile

    @pl.when(block == 0)
    def _():
        acc[...] = jnp.zeros_like(acc)
        top[...] = jnp.full_like(top, LOW)
        for h in range(2):
            values[h, :, WIDTH:] = jnp.ones((KEY_BLOCK, WIDTH), BF)

    wide[...] = x_ref[...].astype(F32)
    for h in range(2):
        keys[h] = wide[pl.ds(2 * h, KEY_BLOCK, stride=4), :].astype(BF)
        values[h, :, :WIDTH] = wide[pl.ds(2 * h + 1, KEY_BLOCK, stride=4), :].astype(BF)

    def score(h, t):
        first = h * 8 + t * per_tile
        q = jnp.concatenate(
            [
                q_ref[:, pl.ds(pl.multiple_of((first + j) * WIDTH, WIDTH), WIDTH)]
                for j in range(per_tile)
            ],
            axis=0,
        )
        return lax.dot_general(q, keys[h], (((1,), (1,)), ((), ())), preferred_element_type=F32)

    def absorb(h, t, s):
        i = h * tiles + t
        before = top[i]
        after = jnp.maximum(before, jnp.max(s, axis=1, keepdims=True) * SCALE)
        top[i] = after
        fade = jnp.exp2(before - after)
        p = jnp.exp2(s * SCALE - after[:, :1]).astype(BF)
        acc[i] = acc[i] * jnp.concatenate([fade, fade], axis=1) + jnp.dot(
            p, values[h], preferred_element_type=F32
        )

    def turn(k, _):
        h, start = k // (tiles // BODY), k % (tiles // BODY) * BODY
        ahead = []
        for t in range(0, BODY, 2):
            now = [(start + u, score(h, start + u)) for u in (t, t + 1)]
            for job in ahead:
                absorb(h, *job)
            ahead = now
        for job in ahead:
            absorb(h, *job)
        return 0

    lax.fori_loop(0, 2 * tiles // BODY, turn, 0, unroll=unroll)

    @pl.when(block == pl.num_programs(0) - 1)
    def _():
        half = tokens // 2
        odd = where[PARITY] == 1
        lane = lax.broadcasted_iota(jnp.int32, (tokens, WIDTH), 1)
        logs = jnp.zeros((tokens, WIDTH), F32)
        for h in range(2):
            for t in range(tiles):
                i = h * tiles + t
                total = acc[i, :, WIDTH:]
                mean = (acc[i, :, :WIDTH] / total).astype(BF)
                log = top[i] + jnp.log2(total)
                for j in range(per_tile):
                    n = h * 8 + t * per_tile + j
                    early = mean[j * tokens : j * tokens + half]
                    late = mean[j * tokens + half : (j + 1) * tokens]
                    cols = slice(n * WIDTH, (n + 1) * WIDTH)
                    o_first[:, cols] = jnp.where(odd, late, early)
                    o_second[:, cols] = jnp.where(odd, early, late)
                    logs = jnp.where(lane == n, log[j * tokens : (j + 1) * tokens], logs)
        high = logs.astype(BF).astype(F32)
        middle = (logs - high).astype(BF).astype(F32)
        low = logs - high - middle
        logs = (high + pltpu.roll(middle, 16, 1) + pltpu.roll(low, 32, 1)).astype(BF)
        o_first[:, 16 * WIDTH :] = jnp.where(odd, logs[half:], logs[:half])
        o_second[:, 16 * WIDTH :] = jnp.where(odd, logs[:half], logs[half:])


def attend(where, queries, cache_rows, other):
    tokens, width = NEW_TOK, queries.shape[1]
    blocks = cache_rows.shape[0] // 2 // 4 // KEY_BLOCK
    tiles = 16 * tokens // TILE

    def request(w):
        return 1 - w[HALF] if other else w[HALF]

    o = jax.ShapeDtypeStruct((tokens // 2, width + WIDTH), BF)
    scores = 16 * tokens * blocks * KEY_BLOCK
    return pl.pallas_call(
        functools.partial(attend_kernel, not other),
        grid_spec=pltpu.PrefetchScalarGridSpec(
            num_scalar_prefetch=1,
            grid=(blocks,),
            in_specs=[
                pl.BlockSpec((tokens, width), lambda i, w: (request(w), 0)),
                pl.BlockSpec((KEY_BLOCK * 4, WIDTH), lambda i, w: (request(w) * blocks + i, 0)),
            ],
            out_specs=[pl.BlockSpec(o.shape, lambda i, w: (0, 0))] * 2,
            scratch_shapes=[
                pltpu.VMEM((tiles, TILE, 2 * WIDTH), F32),
                pltpu.VMEM((tiles, TILE, WIDTH), F32),
                pltpu.VMEM((KEY_BLOCK * 4, WIDTH), F32),
                pltpu.VMEM((2, KEY_BLOCK, WIDTH), BF),
                pltpu.VMEM((2, KEY_BLOCK, 2 * WIDTH), BF),
            ],
        ),
        out_shape=[o, o],
        compiler_params=pltpu.CompilerParams(vmem_limit_bytes=ATTEND_VMEM),
        cost_estimate=pl.CostEstimate(
            flops=scores * WIDTH * 8, bytes_accessed=5 * 2**20, transcendentals=scores
        ),
        name="attend_other" if other else "attend_own",
    )(where, queries, cache_rows)


def owner(where, plane, r):
    return where[ADAPTERS + 2 * (2 * plane + where[CORE]) + r]


def when_mine(where, adapter, maps, out, sem):
    down, up, mate_down, mate_up = maps
    mine = adapter // 8 == where[PLANE]
    mates = adapter // 4 % 2 != where[CORE]
    k = adapter % 4
    depth = down.shape[1]
    cols = pl.ds(pl.multiple_of(where[PARITY] * WIDTH, WIDTH), WIDTH)

    def pair(downs, ups):
        return (
            pltpu.make_async_copy(downs.at[k], out.at[:depth], sem.at[0]),
            pltpu.make_async_copy(ups.at[k, where[HALF], :, cols], out.at[depth:], sem.at[1]),
        )

    def start():
        @pl.when(jnp.logical_and(mine, mates))
        def _():
            for copy in pair(mate_down, mate_up):
                copy.start()

        @pl.when(jnp.logical_and(mine, jnp.logical_not(mates)))
        def _():
            for copy in pair(down, up):
                copy.start()

    def wait():
        @pl.when(mine)
        def _():
            for copy in pair(down, up):
                copy.wait()

    return mine, start, wait


def relay_kernel(slots, arrivals, where, *refs):
    maps, came, outs, sem = refs[:4], refs[4 : 4 + arrivals], refs[4 + arrivals : -1], refs[-1]
    waits = []
    for n, (way, slot, hops, r, arrival) in enumerate(slots):
        plane = lax.rem(where[PLANE] + hops + 8, 8)
        out = outs[way].at[slot]
        mine, start, wait = when_mine(where, owner(where, plane, r), maps, out, sem.at[n])
        start()
        waits.append(wait)
        if arrival is not None:

            @pl.when(jnp.logical_not(mine))
            def _(out=out, arrival=arrival):
                out[...] = came[arrival[0]][arrival[1]]

    for wait in waits:
        wait()


def relay(where, maps, came, slots, name):
    height = maps[0].shape[1] + maps[1].shape[2]
    ways = 1 + max(slot[0] for slot in slots)
    outs = [
        jax.ShapeDtypeStruct((sum(slot[0] == way for slot in slots), height, WIDTH), BF)
        for way in range(ways)
    ]
    anywhere = pl.BlockSpec(memory_space=pl.ANY)
    whole = pl.BlockSpec(memory_space=pltpu.VMEM)
    return pl.pallas_call(
        functools.partial(relay_kernel, slots, len(came)),
        in_specs=[pl.BlockSpec(memory_space=pltpu.SMEM)] + [anywhere] * 4 + [whole] * len(came),
        out_specs=[whole] * ways,
        out_shape=outs,
        scratch_shapes=[pltpu.SemaphoreType.DMA((len(slots), 2))],
        compiler_params=pltpu.CompilerParams(vmem_limit_bytes=SMALL_VMEM),
        cost_estimate=pl.CostEstimate(
            flops=0, bytes_accessed=2 * 2**20, transcendentals=0
        ),
        name=name,
    )(where, *map(in_hbm, maps[:2]), *maps[2:], *came)


def rank_kernel(where, hidden_ref, *refs):
    maps, came, (rank_out, up_out, held, sem) = refs[:4], refs[4:8], refs[8:]
    depth = hidden_ref.shape[1]
    waits = []
    for r in range(2):
        adapter = owner(where, where[PLANE], r)
        _, start, wait = when_mine(where, adapter, maps, held.at[r], sem.at[r])
        start()
        waits.append(wait)
        away = lax.rem(where[PLANE] + 8 - adapter // 8, 8)
        odd = away % 2 == 1
        below = away <= 4 if r == 0 else away < 4
        above = jnp.logical_not(below)
        even = jnp.logical_and(away != 0, jnp.logical_not(odd))
        for source, chosen in zip(
            came,
            (
                jnp.logical_and(odd, below),
                jnp.logical_and(even, below),
                jnp.logical_and(odd, above),
                jnp.logical_and(even, above),
            ),
        ):

            @pl.when(chosen)
            def _(r=r, source=source):
                held[r] = source[r]

    for r in range(2):
        waits[r]()
        rank_out[r * NEW_TOK : (r + 1) * NEW_TOK] = jnp.dot(
            hidden_ref[r * NEW_TOK : (r + 1) * NEW_TOK],
            held[r, :depth],
            preferred_element_type=F32,
        ).astype(BF)
        up_out[r] = held[r, depth:]


def rank_parts(where, hidden, maps, came):
    height = came[0].shape[1]
    anywhere = pl.BlockSpec(memory_space=pl.ANY)
    whole = pl.BlockSpec(memory_space=pltpu.VMEM)
    return pl.pallas_call(
        rank_kernel,
        in_specs=[pl.BlockSpec(memory_space=pltpu.SMEM), whole]
        + [anywhere] * 4
        + [whole] * 4,
        out_specs=[whole, whole],
        out_shape=[
            jax.ShapeDtypeStruct((hidden.shape[0], WIDTH), BF),
            jax.ShapeDtypeStruct((2, height - hidden.shape[1], WIDTH), BF),
        ],
        scratch_shapes=[pltpu.VMEM((2, height, WIDTH), BF), pltpu.SemaphoreType.DMA((2, 2))],
        compiler_params=pltpu.CompilerParams(vmem_limit_bytes=SMALL_VMEM),
        name="rank_partial",
    )(where, hidden, *map(in_hbm, maps[:2]), *maps[2:], *came)


def parcel_kernel(where, base_ref, got_ref, up_ref, *refs):
    ranks, outs = refs[:4], refs[4:]
    after = NEW_TOK + up_ref.shape[1]
    half = where[HALF]
    for out, request in zip(outs, (half, 1 - half)):
        rows = pl.ds(pl.multiple_of(request * NEW_TOK, NEW_TOK), NEW_TOK)
        out[:NEW_TOK] = sum(rank[rows].astype(F32) for rank in ranks).astype(BF)
        out[NEW_TOK:after] = up_ref[request]
    rows = pl.ds(pl.multiple_of(half * NEW_TOK, NEW_TOK), NEW_TOK)
    for part in range(4):
        start = after + part * NEW_TOK
        cols = slice(part * WIDTH, (part + 1) * WIDTH)
        outs[0][start : start + NEW_TOK] = (
            base_ref[rows, cols].astype(F32) + got_ref[:, cols].astype(F32)
        ).astype(BF)


def parcels(where, base, got, ups, ranks):
    whole = pl.BlockSpec(memory_space=pltpu.VMEM)
    height = NEW_TOK + ups.shape[1]
    return pl.pallas_call(
        parcel_kernel,
        in_specs=[pl.BlockSpec(memory_space=pltpu.SMEM)] + [whole] * 7,
        out_specs=[whole, whole],
        out_shape=[
            jax.ShapeDtypeStruct((height + 4 * NEW_TOK, WIDTH), BF),
            jax.ShapeDtypeStruct((height, WIDTH), BF),
        ],
        compiler_params=pltpu.CompilerParams(vmem_limit_bytes=SMALL_VMEM),
        name="tensor_sum",
    )(where, base, got, ups, *ranks)


def merge_kernel(*refs):
    parts, mean_out, log_out = refs[:4], refs[4], refs[5]
    half = parts[0].shape[0]
    tops = []
    for part in parts:
        packed = part[:, 16 * WIDTH :].astype(F32)
        tops.append(packed + pltpu.roll(packed, WIDTH - 16, 1) + pltpu.roll(packed, WIDTH - 32, 1))
    top = functools.reduce(jnp.maximum, tops)
    weights = [jnp.exp2(l - top) for l in tops]
    total = sum(weights)
    merged = top + jnp.log2(total)
    weights = [w / total for w in weights]
    for n in range(16):
        rows = slice(n * half, (n + 1) * half)
        cols = slice(n * WIDTH, (n + 1) * WIDTH)
        mean_out[rows] = sum(
            w[:, n : n + 1] * part[:, cols].astype(F32) for w, part in zip(weights, parts)
        )
        log_out[rows] = jnp.broadcast_to(merged[:, n : n + 1], (half, WIDTH))


def merge(parts):
    out = jax.ShapeDtypeStruct((16 * parts[0].shape[0], WIDTH), F32)
    whole = pl.BlockSpec(memory_space=pltpu.VMEM)
    return pl.pallas_call(
        merge_kernel,
        in_specs=[whole] * 4,
        out_specs=[whole, whole],
        out_shape=[out, out],
        compiler_params=pltpu.CompilerParams(vmem_limit_bytes=SMALL_VMEM),
        name="merge_prefix",
    )(*parts)


def final_kernel(where, q_ref, cos_ref, sin_ref, mean_ref, log_ref, *rest):
    parts, (kv_out, attention_out, wide, up_ref) = rest[:4], rest[4:]
    half = q_ref.shape[0]
    start = pl.multiple_of(where[PARITY] * half, half)
    after = NEW_TOK + up_ref.shape[1]
    rank = sum(part[:NEW_TOK].astype(F32) for part in parts).astype(BF)
    for step, part in enumerate(parts):
        up_ref[jnp.bitwise_xor(where[SEQ], step)] = part[NEW_TOK:after]
    base = [
        sum(
            part[after + col * NEW_TOK : after + (col + 1) * NEW_TOK].astype(F32)
            for part in parts[:2]
        )
        for col in range(4)
    ]
    keys, values = [], []
    for h in range(2):
        for e in range(2):
            delta = jnp.dot(
                rank[:, e * 64 : (e + 1) * 64], up_ref[2 * e + h], preferred_element_type=F32
            )
            part = 2 * h + e
            field = base[part] + delta
            if e == 0:
                field = field * cos_ref[...] + pltpu.roll(field, WIDTH // 2, 1) * sin_ref[...]
            wide[pl.ds(part, NEW_TOK, stride=4), :] = field
            (keys, values)[e].append(field.astype(BF))
    kv_out[...] = wide[pl.ds(start * 4, half * 4), :].astype(BF)
    rows = 8 * half
    token = lax.broadcasted_iota(jnp.int32, (rows, NEW_TOK), 0) % half + start
    seen = lax.broadcasted_iota(jnp.int32, (rows, NEW_TOK), 1) <= token
    ones = jnp.ones((NEW_TOK, WIDTH), BF)
    for h in range(2):
        q = jnp.concatenate(
            [q_ref[:, n * WIDTH : (n + 1) * WIDTH] for n in range(h * 8, h * 8 + 8)], axis=0
        )
        s = lax.dot_general(q, keys[h], (((1,), (1,)), ((), ())), preferred_element_type=F32)
        s = jnp.where(seen, s * SCALE, LOW)
        block = slice(h * rows, (h + 1) * rows)
        log = log_ref[block]
        top = jnp.maximum(log, jnp.max(s, axis=1, keepdims=True))
        weight = jnp.exp2(log - top)
        p = jnp.exp2(s - top).astype(BF)
        value = jnp.dot(
            p, jnp.concatenate([values[h], ones], axis=1), preferred_element_type=F32
        )
        out = (value[:, :WIDTH] + weight * mean_ref[block]) / (value[:, WIDTH:] + weight)
        out = out.astype(BF)
        for j in range(8):
            n = h * 8 + j
            attention_out[:, n * WIDTH : (n + 1) * WIDTH] = out[j * half : (j + 1) * half]


def final(where, queries, cos, sin, mean, log, parts):
    half, width = NEW_TOK // 2, queries.shape[1]

    def whole(a):
        return pl.BlockSpec(a.shape, lambda i, w: (0,) * a.ndim)

    rest = [cos, sin, mean, log, *parts]
    return pl.pallas_call(
        final_kernel,
        grid_spec=pltpu.PrefetchScalarGridSpec(
            num_scalar_prefetch=1,
            grid=(1,),
            in_specs=[pl.BlockSpec((half, width), lambda i, w: (w[SEQ], 0))]
            + [whole(a) for a in rest],
            out_specs=[
                pl.BlockSpec((half * 4, WIDTH), lambda i, w: (0, 0)),
                pl.BlockSpec((half, width), lambda i, w: (0, 0)),
            ],
            scratch_shapes=[
                pltpu.VMEM((NEW_TOK * 4, WIDTH), F32),
                pltpu.VMEM((4, parts[0].shape[0] - 5 * NEW_TOK, WIDTH), BF),
            ],
        ),
        out_shape=[
            jax.ShapeDtypeStruct((half * 4, WIDTH), BF),
            jax.ShapeDtypeStruct((half, width), BF),
        ],
        compiler_params=pltpu.CompilerParams(vmem_limit_bytes=SMALL_VMEM),
        name="new_kv_and_attention",
    )(where, queries, *rest)


def rotary_tables():
    exponents = jnp.arange(WIDTH // 2, dtype=F32)
    frequency = jnp.exp(exponents * (-2.0 * math.log(500000.0) / WIDTH))
    positions = CACHE + jnp.arange(NEW_TOK, dtype=jnp.int32)
    angles = positions.astype(F32)[:, None] * frequency[None, :]
    cos, sin = jnp.cos(angles), jnp.sin(angles)
    return jnp.concatenate([cos, cos], axis=1), jnp.concatenate([-sin, sin], axis=1)


def flip(axis, mask):
    return lambda a: lax.ppermute(
        a, axis, [(i, i ^ mask) for i in range(lax.axis_size(axis))]
    )


def shift(axis, step):
    size = lax.axis_size(axis)
    return lambda a: lax.ppermute(a, axis, [(i, (i + step) % size) for i in range(size)])


def tie(value, *others):
    return lax.optimization_barrier((value, *others))[0]


def local(
    hidden,
    key_value_weight,
    adapter_down_weight,
    adapter_up_weight,
    queries,
    key_value_cache,
    request_adapter,
):
    seq, group, tensor = (lax.axis_index(a) for a in ("seq", "group", "tensor"))
    place = jnp.stack([seq, seq // 2, seq % 2, tensor, group // 2, group % 2])
    where = jnp.concatenate([place.astype(jnp.int32), request_adapter])

    maps = [adapter_down_weight, adapter_up_weight]
    maps += [flip("group", 1)(a) for a in maps]

    far = [(0, 0, 3, 0, None), (0, 1, 3, 1, None), (0, 2, 4, 0, None)]
    far += [(1, 0, -3, 0, None), (1, 1, -3, 1, None), (1, 2, -4, 1, None)]
    two = [(0, 0, 2, 0, (0, 2)), (0, 1, 2, 1, None), (1, 0, -2, 0, None), (1, 1, -2, 1, (1, 2))]
    one = [(0, 0, 1, 0, (0, 0)), (0, 1, 1, 1, (0, 1)), (1, 0, -1, 0, (1, 0)), (1, 1, -1, 1, (1, 1))]

    sent = relay(where, maps, [], far, "relay_far")
    came = [shift("group", 4)(sent[0]), shift("group", -4)(sent[1])]

    cache_rows = key_value_cache.reshape(-1, WIDTH)
    *parts, cache_rows, queries = prep(
        tie(where, *sent), hidden, key_value_weight.reshape(-1, WIDTH), cache_rows, queries
    )
    received = [shift("tensor", step)(parts[step]) for step in (1, 2, 3)]
    o2, o3 = attend(tie(where, parts[0]), queries, cache_rows, True)

    twos = relay(tie(where, o2), maps, came, two, "relay_two")
    two_up, two_down = shift("group", 4)(twos[0]), shift("group", -4)(twos[1])
    ones = relay(tie(where, *twos), maps, came, one, "relay_one")
    came = [shift("group", 2)(ones[0]), two_up, shift("group", -2)(ones[1]), two_down]
    sent = [*twos, *ones]
    received = lax.optimization_barrier((*received, *sent))[:3]
    base = (parts[0].astype(F32) + sum(r.astype(F32) for r in received)).astype(BF)
    got2 = flip("seq", 2)(tie(o2, *sent))
    base_other = lax.dynamic_slice_in_dim(base, (1 - seq // 2) * NEW_TOK, NEW_TOK, 0)
    o0, o1 = attend(tie(where, *sent, base, base_other), queries, cache_rows, False)
    got_base = flip("seq", 3)(tie(base_other, o1))

    cos, sin = rotary_tables()
    rank, ups = rank_parts(tie(where, o1, cos, sin, got2), hidden, maps, came)
    got1, got3 = flip("seq", 1)(tie(o1, rank)), flip("seq", 3)(tie(o3, rank))
    ranks = [rank] + [shift("tensor", step)(rank) for step in (1, 2, 3)]
    mine, others = parcels(where, base, got_base, ups, ranks)
    parts = [mine, flip("seq", 1)(mine), flip("seq", 2)(others), flip("seq", 3)(others)]
    mean, log = merge(list(lax.optimization_barrier((o0, got1, got2, got3, mine)))[:4])

    new_kv, attention = final(where, queries, cos, sin, mean, log, parts)
    return new_kv.reshape(-1, 2, 2, WIDTH), attention


def solution(mesh):
    in_specs = (
        P("group", ("tensor", "seq")),
        P(("tensor", "seq"), None, None, None),
        P("group", ("tensor", "seq"), None),
        P("group", None, None, "tensor"),
        P("group", "tensor"),
        P("group", "seq", "tensor", None, None),
        P(),
    )
    out_specs = (P(("group", "seq"), "tensor", None, None), P(("group", "seq"), "tensor"))
    return jax.shard_map(local, mesh=mesh, in_specs=in_specs, out_specs=out_specs, check_vma=False)
```
